256 devices in a mesh: rows: 128 (over x, z, y), sub: 2 (over core).
Axes of the slice: x: 4, y: 4, z: 8, core: 2. Of those that a mesh axis runs over, the one named last changes fastest.
Arguments:
- upper_tiles: bfloat16 [8192, 64, 256], P('rows', None, 'sub'), may hold values from 0 to 1
- tile_clusters: int32 [8192, 4], P('rows', 'sub'), may hold values from 0 to 8191, as said below
- cluster_slot: int32 [8192], replicated, may hold values from 0 to 8191, as said below
- start_block: float32 [16, 524288], P('sub', 'rows'), may hold values from -6 to 6
Outputs:
- basis: float32 [2, 16, 524288], P(None, 'sub', 'rows')
- coefficients: float32 [4, 16, 16], replicated
The draws below stay inside these ranges and needn't reach their ends.
Inputs may be any that keep to these rules, and one draw needn't show every extreme that they name: `cluster_slot`: a permutation of 0 to 8191. `tile_clusters`: for each index of rows and each tile pair (tiles 0 and 1, or 2 and 3) of its block rows, at most 3 tiles have their column block cluster_slot[id] on rows index cluster_slot[id] // 64; some such count equals 3.
All inputs are finite; a program needn't handle non-finite values.
Results may differ from the reference program's by a relative error of at most 0.0029.
Values may be sent and summed in bfloat16 or wider, within the bound.
A program may use at most 64 MiB of HBM per device.

```python
import math
import jax
import jax.numpy as jnp
from jax import lax

CL = 64
K = 16
STEPS = 2
BLK_DEV = 64
CAP = 3
BLOCKS = 8192
NODES = 524288
N_ROWS = 128


def routing(key):
    key_order, key_slots, key_local = jax.random.split(key, 3)
    ordering = jax.random.permutation(key_order, BLOCKS).astype(jnp.int32)
    total = N_ROWS * CAP

    def one_group(group_key):
        key_score, key_pin = jax.random.split(group_key)
        scores = jax.random.permutation(key_score, total).astype(jnp.int32)
        pinned = jax.random.randint(key_pin, (), 0, N_ROWS, dtype=jnp.int32)
        slot_ids = jnp.arange(total, dtype=jnp.int32)
        scores = jnp.where(slot_ids // CAP == pinned, slot_ids % CAP - CAP, scores)
        taken = jnp.argsort(scores)[:2 * BLK_DEV].astype(jnp.int32)
        return taken // CAP
    group_keys = jax.random.split(key_slots, N_ROWS * 2)
    destination = jax.vmap(one_group)(group_keys)
    local_block = jax.random.randint(key_local, (N_ROWS * 2, 2 * BLK_DEV), 0, BLK_DEV, dtype=jnp.int32)
    position = destination * BLK_DEV + local_block
    inverse = jnp.argsort(ordering).astype(jnp.int32)
    clusters = inverse[position]
    clusters = clusters.reshape(N_ROWS, 2, BLK_DEV, 2).transpose(0, 2, 1, 3).reshape(BLOCKS, 4)
    return (ordering, clusters)


def draw_cluster_slot(key, part):
    shared = routing(key)
    return shared[0]


def draw_tile_clusters(key, part):
    shared = routing(key)
    return shared[1]


def level_of(key, extent, cuts, smallest, high):
    def one(dim, parts):
        steps = jax.random.uniform(jax.random.fold_in(jax.random.fold_in(key, 6), dim), (parts,), jnp.float32, smallest / len(cuts), high / len(cuts))
        return jnp.repeat(jnp.exp(steps), extent[dim] // parts).reshape((-1,) + (1,) * (len(extent) - dim - 1))

    factor_of = one(*cuts[0])
    for cut in cuts[1:]:
        factor_of = factor_of * one(*cut)
    return factor_of


def bell_draw(stream_key, shape, scale, reach, shards=(), kind=jnp.bfloat16):
    array = scale * jax.random.normal(stream_key, shape, jnp.float32)
    if shards:
        array = array * level_of(stream_key, shape, shards, -0.22, 0.18)
    return jnp.clip(array, -reach, reach).astype(kind)


def setup_inputs(seed: int = 0) -> dict:
    splits = jax.random.split(jax.random.key(seed), 5)
    upper_tiles = jnp.clip(1.0 * jax.random.uniform(splits[0], (BLOCKS, CL, 4 * CL), jnp.float32) ** level_of(splits[0], (BLOCKS, CL, 4 * CL), ((0, 128), (2, 2)), -0.2, 0.2), 0.0, 1.0).astype(jnp.bfloat16)
    tile_clusters = draw_tile_clusters(jax.random.fold_in(splits[4], 71), 0)
    cluster_slot = draw_cluster_slot(jax.random.fold_in(splits[4], 71), 0)
    start_block = bell_draw(splits[3], (K, NODES), 1.0, 6.0, ((0, 2), (1, 128)), jnp.float32)
    return {"upper_tiles": upper_tiles, "tile_clusters": tile_clusters, "cluster_slot": cluster_slot, "start_block": start_block}


def inner(left, right):
    return jnp.dot(left, right.T, precision=lax.Precision.HIGHEST)

def times(left, right):
    return jnp.dot(left, right, precision=lax.Precision.HIGHEST)

def weighted_degrees(upper_tiles, column_pos):
    degree = jnp.zeros((BLOCKS, CL), jnp.float32)
    for tile_idx in range(4):
        tile = upper_tiles[:, :, tile_idx * CL:(tile_idx + 1) * CL]
        degree = degree + lax.optimization_barrier(jnp.sum(tile, axis=2, dtype=jnp.float32))
        column_total = lax.optimization_barrier(jnp.sum(tile, axis=1, dtype=jnp.float32))
        degree = degree.at[column_pos[:, tile_idx]].add(column_total)
    return degree.reshape(NODES)

def operate(vectors, upper_tiles, column_pos, scale):
    scaled = (vectors * scale[None, :]).astype(jnp.bfloat16)
    blocked = scaled.reshape(K, BLOCKS, CL).transpose(1, 0, 2).astype(jnp.float32)
    total = jnp.zeros((BLOCKS, K, CL), jnp.float32)
    for tile_idx in range(4):
        tile = upper_tiles[:, :, tile_idx * CL:(tile_idx + 1) * CL].astype(jnp.float32)
        partner = blocked[column_pos[:, tile_idx]]
        total = total + jnp.einsum('ekc,erc->ekr', partner, tile)
        mirrored = jnp.einsum('ekr,erc->ekc', blocked, tile)
        total = total.at[column_pos[:, tile_idx]].add(mirrored)
    product = total.transpose(1, 0, 2).reshape(K, NODES)
    return vectors - scale[None, :] * product

def reference(upper_tiles, tile_clusters, cluster_slot, start_block):
    column_pos = cluster_slot[tile_clusters].astype(jnp.int32)
    scale = lax.rsqrt(weighted_degrees(upper_tiles, column_pos))
    first = inner(start_block, start_block)
    lower = jnp.linalg.cholesky(first)
    current = lax.linalg.triangular_solve(lower, start_block, left_side=True, lower=True)
    previous = jnp.zeros_like(current)
    link = jnp.zeros((K, K), jnp.float32)
    bases = []
    coeffs = []
    for step in range(STEPS):
        applied = operate(current, upper_tiles, column_pos, scale)
        alpha = inner(current, applied)
        residual = applied - times(alpha.T, current) - times(link.T, previous)
        gram = inner(residual, residual)
        lower = jnp.linalg.cholesky(gram)
        following = lax.linalg.triangular_solve(lower, residual, left_side=True, lower=True)
        coeffs.append(alpha)
        coeffs.append(lower.T)
        bases.append(following * math.sqrt(NODES))
        previous, current, link = (current, following, lower)
    return (jnp.stack(bases), jnp.stack(coeffs))
```

```python
import math

import jax
import jax.numpy as jnp
from jax import lax
from jax.experimental import pallas as pl
from jax.experimental.pallas import tpu as pltpu
from jax.sharding import PartitionSpec as P

STEPS = 2
MESH = pl.DeviceIdType.MESH
VMEM = pl.BlockSpec(memory_space=pltpu.VMEM)


def inner(left, right):
    return jnp.dot(left, right.T, precision=lax.Precision.HIGHEST)


def times(left, right):
    return jnp.dot(left, right, precision=lax.Precision.HIGHEST)


def exchange_kernel(in_ref, out_ref, send_sem, recv_sem, local_sem):
    groups = in_ref.shape[0]
    me, sub = lax.axis_index("rows"), lax.axis_index("sub")
    barrier = pltpu.get_barrier_semaphore()

    def greet(i, carry):
        peer = lax.rem(me + i, groups)
        pl.semaphore_signal(barrier, inc=1, device_id=(peer, sub), device_id_type=MESH)
        return carry

    lax.fori_loop(1, groups, greet, 0)
    own = pltpu.make_async_copy(in_ref.at[me], out_ref.at[me], local_sem)
    own.start()
    pl.semaphore_wait(barrier, groups - 1)

    def send(i, carry):
        peer = lax.rem(me + i, groups)
        pltpu.make_async_remote_copy(
            src_ref=in_ref.at[peer],
            dst_ref=out_ref.at[me],
            send_sem=send_sem,
            recv_sem=recv_sem,
            device_id=(peer, sub),
            device_id_type=MESH,
        ).start()
        return carry

    lax.fori_loop(1, groups, send, 0)
    own.wait()
    rest = pl.ds(0, groups - 1)
    pltpu.make_async_remote_copy(
        src_ref=in_ref.at[rest],
        dst_ref=out_ref.at[rest],
        send_sem=send_sem,
        recv_sem=recv_sem,
        device_id=(lax.rem(me + 1, groups), sub),
        device_id_type=MESH,
    ).wait()


def exchange(x, ident):
    return pl.pallas_call(
        exchange_kernel,
        out_shape=jax.ShapeDtypeStruct(x.shape, x.dtype),
        in_specs=[VMEM],
        out_specs=VMEM,
        scratch_shapes=[pltpu.SemaphoreType.DMA] * 3,
        compiler_params=pltpu.CompilerParams(
            collective_id=ident, has_side_effects=True, vmem_limit_bytes=32 << 20
        ),
    )(x)


def total_kernel(sizes, x_ref, o_ref, near, far, send_sem, recv_sem):
    nx, nz, ny = sizes
    me, sub = lax.axis_index("rows"), lax.axis_index("sub")
    x, z, y = me // (nz * ny), lax.rem(me // ny, nz), lax.rem(me, ny)

    def device(x, z, y):
        return ((lax.rem(x, nx) * nz + lax.rem(z, nz)) * ny + lax.rem(y, ny), sub)

    plane = [device(x + a, z, y + b) for a in range(nx) for b in range(ny)][1:]
    line = [device(x, z + a, y) for a in range(1, nz)]
    barrier = pltpu.get_barrier_semaphore()
    for peer in plane + line:
        pl.semaphore_signal(barrier, inc=1, device_id=peer, device_id_type=MESH)
    pl.semaphore_wait(barrier, len(plane) + len(line))
    current = x_ref[...]
    for k, (slots, place, peers) in enumerate(((near, x * ny + y, plane), (far, z, line))):
        slots[pl.ds(place, 1)] = current[None]
        for peer in peers:
            pltpu.make_async_remote_copy(
                src_ref=slots.at[place],
                dst_ref=slots.at[place],
                send_sem=send_sem.at[k],
                recv_sem=recv_sem.at[k],
                device_id=peer,
                device_id_type=MESH,
            ).start()
        others = pl.ds(0, len(peers))
        pltpu.make_async_remote_copy(
            src_ref=slots.at[others],
            dst_ref=slots.at[others],
            send_sem=send_sem.at[k],
            recv_sem=recv_sem.at[k],
            device_id=peers[0],
            device_id_type=MESH,
        ).wait()
        current = jnp.sum(slots[...], axis=0)
    o_ref[...] = current


def total(x, ident):
    k = x.shape[0]
    padded = jnp.pad(x, ((0, 0), (0, 128 - k)))
    out = pl.pallas_call(
        lambda *refs: total_kernel((4, 8, 4), *refs),
        out_shape=jax.ShapeDtypeStruct(padded.shape, x.dtype),
        in_specs=[VMEM],
        out_specs=VMEM,
        scratch_shapes=[
            pltpu.VMEM((16,) + padded.shape, x.dtype),
            pltpu.VMEM((8,) + padded.shape, x.dtype),
            pltpu.SemaphoreType.DMA((2,)),
            pltpu.SemaphoreType.DMA((2,)),
        ],
        compiler_params=pltpu.CompilerParams(collective_id=ident, has_side_effects=True),
    )(padded)
    return out[:, :k]


def local(upper_tiles, tile_clusters, cluster_slot, start_block):
    blocks = upper_tiles.shape[0]
    cluster = upper_tiles.shape[1]
    groups = lax.axis_size("rows")
    capacity = 2 * blocks // groups + 2
    per_row = upper_tiles.shape[2] // cluster
    stacked = upper_tiles.reshape(blocks, cluster, per_row, cluster).transpose(0, 2, 1, 3)
    targets = cluster_slot[tile_clusters].reshape(-1)
    owners = targets // blocks
    local_block = targets % blocks
    count = owners.shape[0]
    order = jnp.arange(count, dtype=jnp.int32)
    before = (owners[:, None] == owners[None, :]) & (order[None, :] < order[:, None])
    ranks = jnp.sum(before.astype(jnp.int32), axis=1)
    slots = owners * capacity + ranks
    tile_columns = jnp.sum(stacked, axis=2, dtype=jnp.float32).reshape(count, cluster)
    named = jnp.concatenate([tile_columns, local_block.astype(jnp.float32)[:, None]], axis=1)
    named = jnp.pad(named, ((0, 0), (0, 128 - cluster - 1)))
    column_out = jnp.zeros((groups * capacity, 128), jnp.float32).at[slots].set(named)
    column_back = exchange(column_out.reshape(groups, capacity, 128), 1)
    column_back = column_back.reshape(groups * capacity, 128)
    asked = column_back[:, cluster].astype(jnp.int32)
    own_degree = jnp.sum(stacked, axis=(1, 3), dtype=jnp.float32)
    degree = own_degree.at[asked].add(column_back[:, :cluster])
    degree = lax.psum(degree, "sub")
    scale = lax.rsqrt(degree.reshape(blocks * cluster))
    full_start = lax.all_gather(start_block, "sub", axis=0, tiled=True)
    first = total(inner(full_start, full_start), 4)
    lower = jnp.linalg.cholesky(first)
    current = lax.linalg.triangular_solve(lower, full_start, left_side=True, lower=True)
    previous = jnp.zeros_like(current)
    link = jnp.zeros_like(first)
    nodes = blocks * cluster * groups
    half_rows = start_block.shape[0]
    bases = []
    coeffs = []
    for step in range(STEPS):
        width_k = current.shape[0]
        scaled = (current * scale[None, :]).astype(jnp.bfloat16)
        scaled = scaled.reshape(width_k, blocks, cluster).transpose(1, 0, 2)
        reply = scaled[asked].reshape(groups, capacity * width_k * cluster // 128, 128)
        mirrored = jnp.einsum("bkr,bwrc->bwkc", scaled, stacked, preferred_element_type=jnp.float32)
        mirrored = mirrored.reshape(count, width_k, cluster)
        outgoing = (
            jnp.zeros((groups * capacity, width_k, cluster), jnp.float32).at[slots].set(mirrored)
        )
        outgoing = outgoing.astype(jnp.bfloat16).reshape(reply.shape)
        both = exchange(jnp.concatenate([reply, outgoing], axis=1), 2)
        fetched, returned = jnp.split(both, 2, axis=1)
        fetched = fetched.reshape(groups * capacity, width_k, cluster)
        returned = returned.reshape(groups * capacity, width_k, cluster).astype(jnp.float32)
        partner = fetched[slots].reshape(blocks, per_row, width_k, cluster)
        forward = jnp.einsum("bwkc,bwrc->bkr", partner, stacked, preferred_element_type=jnp.float32)
        summed = forward.at[asked].add(returned)
        product = summed.transpose(1, 0, 2).reshape(width_k, blocks * cluster)
        product = lax.psum(product, "sub")
        applied = current - scale[None, :] * product
        alpha = total(inner(current, applied), 4)
        residual = applied - times(alpha.T, current) - times(link.T, previous)
        gram = total(inner(residual, residual), 4)
        lower = jnp.linalg.cholesky(gram)
        following = lax.linalg.triangular_solve(lower, residual, left_side=True, lower=True)
        coeffs.append(alpha)
        coeffs.append(lower.T)
        own_rows = lax.dynamic_slice_in_dim(
            following, lax.axis_index("sub") * half_rows, half_rows, 0
        )
        bases.append(own_rows * math.sqrt(nodes))
        previous, current, link = (current, following, lower)
    return (jnp.stack(bases), jnp.stack(coeffs))


def solution(mesh):
    in_specs = (P("rows", None, "sub"), P("rows", "sub"), P(), P("sub", "rows"))
    out_specs = (P(None, "sub", "rows"), P())
    return jax.shard_map(local, mesh=mesh, in_specs=in_specs, out_specs=out_specs, check_vma=False)
```

```python
import functools
import math

import jax
import jax.numpy as jnp
from jax import lax
from jax.experimental import pallas as pl
from jax.experimental.pallas import tpu as pltpu
from jax.sharding import PartitionSpec as P

CAP = 3
MESH = pl.DeviceIdType.MESH
VMEM = pl.BlockSpec(memory_space=pltpu.VMEM)
SMEM = pl.BlockSpec(memory_space=pltpu.SMEM)
F32 = jnp.float32
BF16 = jnp.bfloat16
LIMIT = 40 << 20
EXACT = lax.Precision.HIGHEST


def dot(left, right):
    return jnp.dot(left, right, precision=EXACT, preferred_element_type=F32)


def dot_t(left, right):
    dims = (((1,), (1,)), ((), ()))
    return lax.dot_general(left, right, dims, precision=EXACT, preferred_element_type=F32)


def swap(x):
    return pltpu.roll(x, 64, 1)


def is_low(shape):
    return lax.broadcasted_iota(jnp.int32, shape, 1) < 64


def pair_up(first, second):
    low = is_low(first.shape)
    return jnp.where(low, first, swap(second)), jnp.where(low, swap(first), second)


class Place:
    def __init__(self, sizes):
        self.nx, self.nz, self.ny = sizes
        self.groups = self.nx * self.nz * self.ny
        self.me, self.sub = lax.axis_index("rows"), lax.axis_index("sub")
        self.x = self.me // (self.nz * self.ny)
        self.z = lax.rem(self.me // self.ny, self.nz)
        self.y = lax.rem(self.me, self.ny)
        self.other = (self.me, 1 - self.sub)
        nx, nz, ny = sizes
        self.plane = [self.at(a, 0, b, 0) for a in range(nx) for b in range(ny)][1:]
        self.line = [self.at(0, a, 0, s) for a in range(nz) for s in range(2)][1:]
        self.slots = (self.x * ny + self.y, self.z * 2 + self.sub)

    def at(self, dx, dz, dy, ds):
        x, z, y = lax.rem(self.x + dx, self.nx), lax.rem(self.z + dz, self.nz), lax.rem(self.y + dy, self.ny)
        return ((x * self.nz + z) * self.ny + y, lax.rem(self.sub + ds, 2))

    def peer(self, i):
        return (lax.rem(self.me + i, self.groups), self.sub)


def signal(barrier, device):
    pl.semaphore_signal(barrier, inc=1, device_id=device, device_id_type=MESH)


def meet(place, everyone):
    barrier = pltpu.get_barrier_semaphore()
    if everyone:
        def greet(i, carry):
            signal(barrier, place.peer(i))
            return carry

        lax.fori_loop(1, place.groups, greet, 0, unroll=8)
        rest = [d for k, d in enumerate(place.line) if k % 2 == 0]
        count = place.groups - 1 + len(rest)
    else:
        rest = place.plane + place.line
        count = len(rest)
    for device in rest:
        signal(barrier, device)
    return lambda: pl.semaphore_wait(barrier, count)


def remote(src, dst, send_sem, recv_sem, device):
    return pltpu.make_async_remote_copy(
        src_ref=src, dst_ref=dst, send_sem=send_sem, recv_sem=recv_sem, device_id=device, device_id_type=MESH
    )


def total(place, current, near, far, send_sem, recv_sem):
    for k, (held, slot, peers) in enumerate(
        ((near, place.slots[0], place.plane), (far, place.slots[1], place.line))
    ):
        held[pl.ds(slot, 1)] = current[None]
        for device in peers:
            remote(held.at[slot], held.at[slot], send_sem.at[k], recv_sem.at[k], device).start()
        rest = pl.ds(0, len(peers))
        remote(held.at[rest], held.at[rest], send_sem.at[k], recv_sem.at[k], peers[0]).wait()
        current = jnp.sum(held[...], axis=0)
    return current


def total_scratch(sizes):
    nx, nz, ny = sizes
    return [
        pltpu.VMEM((nx * ny, 16, 128), F32),
        pltpu.VMEM((nz * 2, 16, 128), F32),
        pltpu.SemaphoreType.DMA((2,)),
        pltpu.SemaphoreType.DMA((2,)),
    ]


def send_all(place, build, src, dst, send_sem, recv_sem, own_sem):
    me, groups = place.me, place.groups
    build(me)
    own = pltpu.make_async_copy(src.at[me], dst.at[me], own_sem)
    own.start()

    def send(i, carry):
        peer, sub = place.peer(i)
        build(peer)
        remote(src.at[peer], dst.at[me], send_sem, recv_sem, (peer, sub)).start()
        return carry

    lax.fori_loop(1, groups, send, 0, unroll=2)
    rest = pl.ds(0, groups - 1)

    def finish():
        own.wait()
        remote(src.at[rest], dst.at[rest], send_sem, recv_sem, place.peer(1)).wait()

    return finish


def factor(gram):
    n = gram.shape[0]
    row = lax.broadcasted_iota(jnp.int32, (n, n), 0)
    col = lax.broadcasted_iota(jnp.int32, (n, n), 1)
    left = gram
    right = jnp.where(row == col, 1.0, 0.0).astype(F32)
    below = lax.broadcasted_iota(jnp.int32, (n, 1), 0)
    for i in range(n):
        share = jnp.where(below > i, left[:, i : i + 1] / left[i : i + 1, i : i + 1], 0.0)
        right = right - share * right[i : i + 1, :]
        left = left - share * left[i : i + 1, :]
    pivots = jnp.sum(jnp.where(row == col, left, 0.0), axis=1, keepdims=True)
    root = lax.rsqrt(pivots)
    return jnp.where(col >= row, left * root, 0.0), right * root


def widen(x):
    return jnp.concatenate([x, jnp.zeros((x.shape[0], 128 - x.shape[1]), F32)], axis=1)


def prepare_blocks(vectors, scale, tiles, scaled, mirrored, blocks):
    scaled[blocks] = jnp.zeros((8, 128), F32)
    mirrored[2 * blocks] = jnp.zeros((8, 128), F32)

    def step(t, carry):
        lanes = pl.ds(pl.multiple_of(t * 128, 128), 128)
        halves = pair_up(vectors[0:8, lanes], vectors[8:16, lanes])
        for p in range(2):
            b = 2 * t + p
            block = halves[p] * jnp.broadcast_to(scale[pl.ds(b, 1), :], (8, 128))
            scaled[b] = block
            left = jnp.concatenate([block, swap(block)], axis=0)[:, :64].astype(BF16)
            out = jnp.dot(left, tiles[b], preferred_element_type=F32)
            first, second = pair_up(out[0:8], out[8:16])
            mirrored[2 * b] = first
            mirrored[2 * b + 1] = second
        return carry

    lax.fori_loop(0, blocks // 2, step, 0, unroll=4)


def chunk_builder(asked, placed, scaled, mirrored, chunks):
    def build(d):
        parts = [scaled[asked[CAP * d + k]] for k in range(CAP)]
        parts += [mirrored[placed[CAP * d + k]] for k in range(CAP)]
        chunks[d] = jnp.concatenate(parts, axis=0).astype(BF16)

    return build


def open_kernel(
    sizes, blocks, tiles, start, names, placed, received, full, first, own_degree,
    named, chunks, near, far, tsend, trecv, send_sem, recv_sem, own_sem, xsend, xrecv, xown,
):
    place = Place(sizes)
    ready = meet(place, True)
    rows = pl.ds(pl.multiple_of(place.sub * 8, 8), 8)
    keep = pltpu.make_async_copy(start, full.at[rows], xown)
    keep.start()
    named[2 * blocks] = jnp.broadcast_to(names[pl.ds(2 * blocks, 1), :], (8, 128))

    def sums(b, carry):
        tile = tiles[b]
        columns = jnp.dot(jnp.ones((8, 64), BF16), tile, preferred_element_type=F32)
        low = is_low(columns.shape)
        named[2 * b] = jnp.where(low, columns, names[pl.ds(2 * b, 1), :])
        named[2 * b + 1] = jnp.where(low, swap(columns), names[pl.ds(2 * b + 1, 1), :])
        dims = (((1,), (1,)), ((), ()))
        across = lax.dot_general(jnp.ones((8, 128), BF16), tile, dims, preferred_element_type=F32)
        own_degree[pl.ds(b, 1), :] = jnp.concatenate([across, across], axis=1)[0:1]
        return carry

    lax.fori_loop(0, blocks, sums, 0, unroll=4)
    ready()
    swap_rows = remote(start, full.at[rows], xsend, xrecv, place.other)
    swap_rows.start()

    def build(d):
        for k in range(CAP):
            chunks[d, pl.ds(k, 1), :] = named[placed[CAP * d + k]][0:1]

    finish = send_all(place, build, chunks, received, send_sem, recv_sem, own_sem)
    keep.wait()
    swap_rows.wait()
    half = full.shape[1] // 2
    part = full[:, pl.ds(pl.multiple_of(place.sub * half, 128), half)]
    first[...] = total(place, widen(dot_t(part, part)), near, far, tsend, trecv)
    finish()


def degree_kernel(blocks, received, asked, own_degree, degree, acc0, acc1, acc2):
    accs = (acc0, acc1, acc2)
    for acc in accs:
        acc[...] = jnp.zeros_like(acc)

    def add(d, carry):
        rows = received[d]
        for k in range(CAP):
            i = asked[CAP * d + k]
            accs[k][i] = accs[k][i] + jnp.broadcast_to(rows[k : k + 1, :], (8, 128))
        return carry

    lax.fori_loop(0, received.shape[0], add, 0, unroll=4)

    def gather(b, carry):
        summed = acc0[b] + acc1[b] + acc2[b]
        summed = jnp.where(is_low(summed.shape), summed, swap(summed))
        degree[pl.ds(b, 1), :] = own_degree[pl.ds(b, 1), :] + summed[0:1]
        return carry

    lax.fori_loop(0, blocks, gather, 0, unroll=4)


def first_kernel(
    sizes, blocks, tiles, degree, full, first, asked, placed, received, vectors, scale,
    theirs, scaled, mirrored, chunks, send_sem, recv_sem, own_sem, xsend, xrecv,
):
    place = Place(sizes)
    ready = meet(place, True)
    _, inverse = factor(first[:, :16])
    vectors[...] = dot(inverse, full[...])
    ready()
    pair = remote(degree, theirs, xsend, xrecv, place.other)
    pair.start()
    pair.wait()
    scale[...] = lax.rsqrt(degree[...] + theirs[...])
    prepare_blocks(vectors, scale, tiles, scaled, mirrored, blocks)
    build = chunk_builder(asked, placed, scaled, mirrored, chunks)
    send_all(place, build, chunks, received, send_sem, recv_sem, own_sem)()


def apply_kernel(blocks, tiles, received, where, asked, product, held, acc0, acc1, acc2):
    accs = (acc0, acc1, acc2)
    for acc in accs:
        acc[...] = jnp.zeros_like(acc)

    def spread(d, carry):
        chunk = received[d].astype(F32).reshape(2 * CAP, 8, 128)
        held[pl.ds(d * CAP, CAP)] = chunk[:CAP]
        for k in range(CAP):
            i = asked[CAP * d + k]
            accs[k][i] = accs[k][i] + chunk[CAP + k]
        return carry

    lax.fori_loop(0, received.shape[0], spread, 0, unroll=4)

    def forward(b, carry):
        low, high = pair_up(held[where[2 * b]], held[where[2 * b + 1]])
        left = jnp.concatenate([low, high], axis=0).astype(BF16)
        dims = (((1,), (1,)), ((), ()))
        out = lax.dot_general(left, tiles[b], dims, preferred_element_type=F32)
        out = jnp.concatenate([out[0:8], out[8:16]], axis=1)
        product[b] = out + acc0[b] + acc1[b] + acc2[b]
        return carry

    lax.fori_loop(0, blocks, forward, 0, unroll=4)


def step_kernel(sizes, blocks, nodes, last, *refs):
    refs = list(refs)
    product, scale, current, previous, link = refs[:5]
    del refs[:5]
    if not last:
        tiles, asked, placed, received, vectors = refs[:5]
        del refs[:5]
    basis, alpha_out, upper_out = refs[:3]
    theirs, stack, near, far, tsend, trecv, xsend, xrecv = refs[3:11]
    del refs[:11]
    if last:
        (vectors,) = refs
    else:
        scaled, mirrored, chunks, send_sem, recv_sem, own_sem = refs
    place = Place(sizes)
    ready = meet(place, not last)
    stack[16:32] = current[...]
    stack[32:48] = previous[...]
    ready()
    pair = remote(product, theirs, xsend, xrecv, place.other)
    pair.start()
    pair.wait()

    def residual(t, carry):
        lanes = pl.ds(pl.multiple_of(t * 128, 128), 128)
        both = []
        for p in range(2):
            b = 2 * t + p
            both.append((product[b] + theirs[b]) * jnp.broadcast_to(scale[pl.ds(b, 1), :], (8, 128)))
        low, high = pair_up(both[0], both[1])
        stack[0:8, lanes] = low
        stack[8:16, lanes] = high
        return carry

    lax.fori_loop(0, blocks // 2, residual, 0, unroll=4)
    half = current.shape[1] // 2
    part = stack[:, pl.ds(pl.multiple_of(place.sub * half, 128), half)]
    gram = dot_t(part, part)
    packed = widen(jnp.concatenate([gram[0:16], gram[16:32], gram[32:48, 32:48]], axis=1))
    packed = total(place, packed, near, far, tsend, trecv)
    rr, rq, rp, qr, qq, qp, pp = (packed[:, 16 * k : 16 * k + 16] for k in range(7))
    gram = jnp.concatenate(
        [
            jnp.concatenate([rr, rq, rp], axis=1),
            jnp.concatenate([qr, qq, qp], axis=1),
            jnp.concatenate([rp.T, qp.T, pp], axis=1),
        ],
        axis=0,
    )
    alpha = qq - qr
    row = lax.broadcasted_iota(jnp.int32, (16, 16), 0)
    col = lax.broadcasted_iota(jnp.int32, (16, 16), 1)
    eye = jnp.where(row == col, 1.0, 0.0).astype(F32)
    mix = jnp.concatenate([-eye, eye - alpha.T, -link[:, :16]], axis=1)
    upper, inverse = factor(dot_t(dot(mix, gram), mix))
    vectors[...] = dot(dot(inverse, mix), stack[...])
    alpha_out[...] = widen(alpha)
    upper_out[...] = widen(upper)
    rows = pl.ds(pl.multiple_of(place.sub * 8, 8), 8)
    basis[...] = vectors[rows, :] * math.sqrt(nodes)
    if not last:
        prepare_blocks(vectors, scale, tiles, scaled, mirrored, blocks)
        build = chunk_builder(asked, placed, scaled, mirrored, chunks)
        send_all(place, build, chunks, received, send_sem, recv_sem, own_sem)()


def call(kernel, name, ident, outs, scratch, specs, *args):
    params = {"vmem_limit_bytes": LIMIT}
    if ident is not None:
        params |= {"collective_id": ident, "has_side_effects": True}
    return pl.pallas_call(
        kernel,
        out_shape=[jax.ShapeDtypeStruct(*o) for o in outs],
        in_specs=specs,
        out_specs=[VMEM] * len(outs),
        scratch_shapes=scratch,
        compiler_params=pltpu.CompilerParams(**params),
        name=name,
    )(*args)


def local(sizes, upper_tiles, tile_clusters, cluster_slot, start_block):
    blocks, cluster, _ = upper_tiles.shape
    groups = sizes[0] * sizes[1] * sizes[2]
    columns = blocks * cluster
    nodes = columns * groups
    count = 2 * blocks
    targets = cluster_slot[tile_clusters].reshape(-1)
    owners = targets // blocks
    order = jnp.arange(count, dtype=jnp.int32)
    before = (owners[:, None] == owners[None, :]) & (order[None, :] < order[:, None])
    ranks = jnp.sum(before.astype(jnp.int32), axis=1)
    where = owners * CAP + ranks
    placed = jnp.full((groups * CAP,), count, jnp.int32).at[where].set(order)
    ids = jnp.concatenate([targets % blocks, jnp.full((1,), blocks, jnp.int32)])
    names = jnp.broadcast_to(ids.astype(F32)[:, None], (count + 1, 128))

    dma = pltpu.SemaphoreType.DMA
    block = lambda n: pltpu.VMEM((n, 8, 128), F32)
    chunk = (groups, 16 * CAP, 128)
    received, full, first, own_degree = call(
        functools.partial(open_kernel, sizes, blocks), "open", 1,
        [((groups, CAP, 128), F32), ((16, columns), F32), ((16, 128), F32), ((blocks, 128), F32)],
        [block(count + 1), pltpu.VMEM((groups, CAP, 128), F32)] + total_scratch(sizes) + [dma] * 6,
        [VMEM, VMEM, VMEM, SMEM],
        upper_tiles, start_block, names, placed,
    )
    asked = received[:, :, cluster].astype(jnp.int32).reshape(-1)
    (degree,) = call(
        functools.partial(degree_kernel, blocks), "degree", None,
        [((blocks, 128), F32)],
        [block(blocks + 1)] * 3,
        [VMEM, SMEM, VMEM],
        received, asked, own_degree,
    )
    fill = [block(blocks + 1), block(count + 1), pltpu.VMEM(chunk, BF16)]
    received, vectors, scale = call(
        functools.partial(first_kernel, sizes, blocks), "first", 2,
        [(chunk, BF16), ((16, columns), F32), ((blocks, 128), F32)],
        [pltpu.VMEM((blocks, 128), F32)] + fill + [dma] * 5,
        [VMEM, VMEM, VMEM, VMEM, SMEM, SMEM],
        upper_tiles, degree, full, first, asked, placed,
    )
    previous, link = jnp.zeros_like(vectors), jnp.zeros((16, 128), F32)
    bases, coeffs = [], []
    for last in (False, True):
        (product,) = call(
            functools.partial(apply_kernel, blocks), "apply", None,
            [((blocks, 8, 128), F32)],
            [block(groups * CAP)] + [block(blocks + 1)] * 3,
            [VMEM, VMEM, SMEM, SMEM],
            upper_tiles, received, where, asked,
        )
        common = [((8, columns), F32), ((16, 128), F32), ((16, 128), F32)]
        scratch = [block(blocks), pltpu.VMEM((48, columns), F32)] + total_scratch(sizes) + [dma] * 2
        kernel = functools.partial(step_kernel, sizes, blocks, nodes, last)
        args = [product, scale, vectors, previous, link]
        if last:
            basis, alpha, upper = call(
                kernel, "finish", 4, common, scratch + [pltpu.VMEM((16, columns), F32)], [VMEM] * 5, *args
            )
        else:
            received, following, basis, alpha, upper = call(
                kernel, "step", 3,
                [(chunk, BF16), ((16, columns), F32)] + common,
                scratch + fill + [dma] * 3,
                [VMEM] * 6 + [SMEM] * 2,
                *args, upper_tiles, asked, placed,
            )
            previous, vectors, link = vectors, following, upper
        bases.append(basis)
        coeffs += [alpha[:, :16], upper[:, :16]]
    return jnp.stack(bases), jnp.stack(coeffs)


def solution(mesh):
    sizes = (4, 8, 4)
    in_specs = (P("rows", None, "sub"), P("rows", "sub"), P(), P("sub", "rows"))
    out_specs = (P(None, "sub", "rows"), P())
    body = functools.partial(local, sizes)
    return jax.shard_map(body, mesh=mesh, in_specs=in_specs, out_specs=out_specs, check_vma=False)
```

```python
import functools
import math

import jax
import jax.numpy as jnp
from jax import lax
from jax.experimental import pallas as pl
from jax.experimental.pallas import tpu as pltpu
from jax.sharding import PartitionSpec as P

CAP = 3
MESH = pl.DeviceIdType.MESH
VMEM = pl.BlockSpec(memory_space=pltpu.VMEM)
SMEM = pl.BlockSpec(memory_space=pltpu.SMEM)
F32 = jnp.float32
BF16 = jnp.bfloat16
LIMIT = 32 << 20
EXACT = lax.Precision.HIGHEST


def dot(left, right):
    return jnp.dot(left, right, precision=EXACT, preferred_element_type=F32)


def dot_t(left, right):
    dims = (((1,), (1,)), ((), ()))
    return lax.dot_general(left, right, dims, precision=EXACT, preferred_element_type=F32)


def swap(x):
    return pltpu.roll(x, 64, 1)


def is_low(shape):
    return lax.broadcasted_iota(jnp.int32, shape, 1) < 64


def pair_up(first, second):
    low = is_low(first.shape)
    return jnp.where(low, first, swap(second)), jnp.where(low, swap(first), second)


class Place:
    def __init__(self, sizes):
        self.nx, self.nz, self.ny = sizes
        self.groups = self.nx * self.nz * self.ny
        self.me, self.sub = lax.axis_index("rows"), lax.axis_index("sub")
        self.x = self.me // (self.nz * self.ny)
        self.z = lax.rem(self.me // self.ny, self.nz)
        self.y = lax.rem(self.me, self.ny)
        self.other = (self.me, 1 - self.sub)
        nx, nz, ny = sizes
        self.plane = [self.at(a, 0, b, 0) for a in range(nx) for b in range(ny)][1:]
        self.line = [self.at(0, a, 0, s) for a in range(nz) for s in range(2)][1:]
        self.slots = (self.x * ny + self.y, self.z * 2 + self.sub)

    def at(self, dx, dz, dy, ds):
        x, z, y = lax.rem(self.x + dx, self.nx), lax.rem(self.z + dz, self.nz), lax.rem(self.y + dy, self.ny)
        return ((x * self.nz + z) * self.ny + y, lax.rem(self.sub + ds, 2))

    def peer(self, i):
        return (lax.rem(self.me + i, self.groups), self.sub)


def signal(barrier, device):
    pl.semaphore_signal(barrier, inc=1, device_id=device, device_id_type=MESH)


def meet(place, everyone):
    barrier = pltpu.get_barrier_semaphore()
    if everyone:
        def greet(i, carry):
            signal(barrier, place.peer(i))
            return carry

        lax.fori_loop(1, place.groups, greet, 0, unroll=8)
        rest = [d for k, d in enumerate(place.line) if k % 2 == 0]
        count = place.groups - 1 + len(rest)
    else:
        rest = place.plane + place.line
        count = len(rest)
    for device in rest:
        signal(barrier, device)
    return lambda: pl.semaphore_wait(barrier, count)


def remote(src, dst, send_sem, recv_sem, device):
    return pltpu.make_async_remote_copy(
        src_ref=src, dst_ref=dst, send_sem=send_sem, recv_sem=recv_sem, device_id=device, device_id_type=MESH
    )


class Total:
    def __init__(self, place, near, far, send_sem, recv_sem):
        self.hops = ((near, place.slots[0], place.plane), (far, place.slots[1], place.line))
        self.sems = (send_sem, recv_sem)

    def copy(self, k, ref, device):
        return remote(ref, ref, self.sems[0].at[k], self.sems[1].at[k], device)

    def start(self, k, value):
        held, slot, peers = self.hops[k]
        held[pl.ds(slot, 1)] = value[None]
        for device in peers:
            self.copy(k, held.at[slot], device).start()

    def finish(self, k):
        held, _, peers = self.hops[k]
        self.copy(k, held.at[pl.ds(0, len(peers))], peers[0]).wait()
        return jnp.sum(held[...], axis=0)


class Exchange:
    def __init__(self, place, src, dst, send_sem, recv_sem, own_sem, rows=None):
        self.place, self.src, self.dst = place, src, dst
        self.sems, self.own_sem, self.rows = (send_sem, recv_sem), own_sem, rows

    def part(self, ref, i):
        return ref.at[i] if self.rows is None else ref.at[i, self.rows]

    def own(self):
        me = self.place.me
        return pltpu.make_async_copy(self.part(self.src, me), self.part(self.dst, me), self.own_sem)

    def start(self, build, unroll=2):
        place = self.place
        build(place.me)
        self.own().start()

        def send(i, carry):
            device = place.peer(i)
            build(device[0])
            remote(self.part(self.src, device[0]), self.part(self.dst, place.me), *self.sems, device).start()
            return carry

        lax.fori_loop(1, place.groups, send, 0, unroll=unroll)

    def rest(self):
        rest = pl.ds(0, self.place.groups - 1)
        return remote(self.part(self.src, rest), self.part(self.dst, rest), *self.sems, self.place.peer(1))

    def receive(self):
        self.own().wait()
        self.rest().wait_recv()

    def sent(self):
        self.rest().wait_send()

def factor(gram):
    n = gram.shape[0]
    row = lax.broadcasted_iota(jnp.int32, (n, n), 0)
    col = lax.broadcasted_iota(jnp.int32, (n, n), 1)
    left = gram
    right = jnp.where(row == col, 1.0, 0.0).astype(F32)
    below = lax.broadcasted_iota(jnp.int32, (n, 1), 0)
    for i in range(n):
        share = jnp.where(below > i, left[:, i : i + 1] / left[i : i + 1, i : i + 1], 0.0)
        right = right - share * right[i : i + 1, :]
        left = left - share * left[i : i + 1, :]
    pivots = jnp.sum(jnp.where(row == col, left, 0.0), axis=1, keepdims=True)
    root = lax.rsqrt(pivots)
    return jnp.where(col >= row, left * root, 0.0), right * root


def widen(x):
    return jnp.concatenate([x, jnp.zeros((x.shape[0], 128 - x.shape[1]), F32)], axis=1)


def kernel(
    sizes, blocks, nodes, tiles, start, names, out_ids, placed, where, bases, coeffs,
    full, first_stack, second_stack, named, out_columns, in_columns, own_degree, degree, their_degree, scale,
    in_ids, ids, onehot, scaled, mirrored, chunks, received, partners, returned, product, theirs,
    near, far, tsend, trecv, csend, crecv, cown, xsend, xrecv, asend, arecv, aown, isend, irecv, iown, id_sem,
):
    place = Place(sizes)
    ready = meet(place, True)
    groups, sub = place.groups, place.sub
    columns = full.shape[1]
    half = columns // 2
    own_half = pl.ds(pl.multiple_of(sub * half, 128), half)
    own_rows = pl.ds(pl.multiple_of(sub * 8, 8), 8)
    totals = [Total(place, near.at[i], far.at[i], tsend.at[i], trecv.at[i]) for i in range(3)]

    def pair(i, src, dst):
        return remote(src, dst, xsend.at[i], xrecv.at[i], place.other)

    full[own_rows, :] = start[...]
    named[2 * blocks] = jnp.broadcast_to(names[pl.ds(2 * blocks, 1), :], (8, 128))
    scaled[blocks] = jnp.zeros((8, 128), F32)
    mirrored[2 * blocks] = jnp.zeros((8, 128), F32)
    across = (((1,), (1,)), ((), ()))

    def sums(b, carry):
        tile = tiles[b]
        down = jnp.dot(jnp.ones((8, 64), BF16), tile, preferred_element_type=F32)
        low = is_low(down.shape)
        named[2 * b] = jnp.where(low, down, names[pl.ds(2 * b, 1), :])
        named[2 * b + 1] = jnp.where(low, swap(down), names[pl.ds(2 * b + 1, 1), :])
        along = lax.dot_general(jnp.ones((8, 128), BF16), tile, across, preferred_element_type=F32)
        own_degree[pl.ds(b, 1), :] = jnp.concatenate([along, along], axis=1)[0:1]
        return carry

    lax.fori_loop(0, blocks, sums, 0, unroll=4)

    def fill(d, carry):
        for k in range(CAP):
            out_columns[d, pl.ds(k, 1), :] = named[placed[CAP * d + k]][0:1]
        return carry

    lax.fori_loop(0, groups, fill, 0, unroll=4)
    ready()
    swap_rows = pair(0, start, full.at[own_rows])
    swap_rows.start()
    sent_columns = Exchange(place, out_columns, in_columns, csend, crecv, cown)
    sent_columns.start(lambda d: None, unroll=4)
    swap_rows.wait()
    part = full[:, own_half]
    totals[0].start(0, widen(dot_t(part, part)))

    sent_ids = Exchange(place, out_ids, in_ids, isend, irecv, iown)
    sent_ids.start(lambda d: None, unroll=4)

    sent_columns.receive()
    sums_in = jnp.zeros((blocks, 128), F32)
    for k in range(CAP):
        rows = in_columns[:, k, :]
        index = lax.broadcasted_iota(jnp.int32, (blocks, groups), 0).astype(F32)
        match = jnp.where(index == rows.T[64:65, :], 1.0, 0.0).astype(F32)
        onehot[k] = match.astype(BF16)
        sums_in = sums_in + dot(match, rows)
    degree[...] = own_degree[...] + jnp.where(is_low(sums_in.shape), sums_in, swap(sums_in))
    swap_degree = pair(1, degree, their_degree)
    swap_degree.start()
    totals[0].start(1, totals[0].finish(0))
    sent_columns.sent()
    sent_ids.receive()
    id_copy = pltpu.make_async_copy(in_ids, ids, id_sem)
    id_copy.start()
    sent_ids.sent()
    id_copy.wait()
    swap_degree.wait()
    scale[...] = lax.rsqrt(degree[...] + their_degree[...])
    _, inverse = factor(totals[0].finish(1)[:, :16])
    first_stack[16:32] = dot(inverse, full[...])

    def scale_of(b):
        return jnp.broadcast_to(scale[pl.ds(b, 1), :], (8, 128))

    def block_rows(b):
        return pl.ds(pl.multiple_of(b * 8, 8), 8)

    for m, stack in enumerate((first_stack, second_stack)):
        def scale_blocks(t, carry):
            lanes = pl.ds(pl.multiple_of(t * 128, 128), 128)
            pairs = pair_up(stack[16:24, lanes], stack[24:32, lanes])
            for p in range(2):
                scaled[2 * t + p] = pairs[p] * scale_of(2 * t + p)
            return carry

        lax.fori_loop(0, blocks // 2, scale_blocks, 0, unroll=4)

        def mirror(b, carry):
            block = scaled[b]
            left = jnp.concatenate([block, swap(block)], axis=0)[:, :64].astype(BF16)
            out = jnp.dot(left, tiles[b], preferred_element_type=F32)
            mirrored[2 * b], mirrored[2 * b + 1] = pair_up(out[0:8], out[8:16])
            return carry

        def builder(k):
            def build(d):
                parts = []
                for slot in (2 * k, 2 * k + 1):
                    if slot < CAP:
                        parts.append(scaled[jnp.clip(ids[d, 0, slot], 0, blocks)])
                    else:
                        parts.append(mirrored[placed[CAP * d + slot - CAP]])
                chunks[d, pl.ds(16 * k, 16), :] = jnp.concatenate(parts, axis=0).astype(BF16)

            return build

        parts = [
            Exchange(
                place, chunks, received.at[m], asend.at[m, k], arecv.at[m, k], aown.at[m, k], pl.ds(16 * k, 16)
            )
            for k in range(CAP)
        ]
        parts[0].start(builder(0))
        lax.fori_loop(0, blocks, mirror, 0, unroll=4)
        parts[1].start(builder(1))
        parts[2].start(builder(2))
        rest = stack[16:, own_half]
        rest = dot_t(rest, rest)

        parts[0].receive()
        parts[1].receive()

        def spread(d, carry):
            chunk = received[m, d, pl.ds(0, 32), :].astype(F32)
            for k in range(CAP):
                partners[d * CAP + k] = chunk[8 * k : 8 * k + 8]
            returned[pl.ds(pl.multiple_of(d * 24, 8), 8), :] = chunk[24:32]
            return carry

        lax.fori_loop(0, groups, spread, 0, unroll=4)

        def forward(b, carry):
            low, high = pair_up(partners[where[2 * b]], partners[where[2 * b + 1]])
            left = jnp.concatenate([low, high], axis=0).astype(BF16)
            out = lax.dot_general(left, tiles[b], across, preferred_element_type=F32)
            product[block_rows(b), :] = jnp.concatenate([out[0:8], out[8:16]], axis=1)
            return carry

        lax.fori_loop(0, blocks, forward, 0, unroll=4)
        parts[2].receive()

        def spread_last(d, carry):
            chunk = received[m, d, pl.ds(32, 16), :].astype(F32)
            returned[pl.ds(pl.multiple_of(d * 24 + 8, 8), 16), :] = chunk
            return carry

        lax.fori_loop(0, groups, spread_last, 0, unroll=4)
        for j in range(8):
            added = jnp.zeros((blocks, 128), F32)
            for k in range(CAP):
                rows = returned[pl.ds(8 * k + j, groups, stride=24), :].astype(BF16)
                added = added + jnp.dot(onehot[k], rows, preferred_element_type=F32)
            lines = pl.ds(j, blocks, stride=8)
            product[lines, :] = product[lines, :] + added

        height = blocks * 4
        halves = [pl.ds(pl.multiple_of(s * height, 8), height) for s in (1 - sub, sub)]
        swaps = [pair(2 + 2 * m + i, product.at[h], theirs.at[m, h]) for i, h in enumerate(halves)]
        for one in swaps:
            one.start()
        for part in parts:
            part.sent()

        def residual(first):
            def step(t, carry):
                t = first + t
                lanes = pl.ds(pl.multiple_of(t * 128, 128), 128)
                both = []
                for p in range(2):
                    b = 2 * t + p
                    both.append((product[block_rows(b), :] + theirs[m, block_rows(b), :]) * scale_of(b))
                stack[0:8, lanes], stack[8:16, lanes] = pair_up(both[0], both[1])
                return carry

            lax.fori_loop(0, blocks // 4, step, 0, unroll=4)

        swaps[0].wait()
        residual(sub * (blocks // 4))
        cross = dot_t(stack[0:16, own_half], stack[:, own_half])
        packed = [cross, rest[0:16]] + ([rest[16:32, 16:32]] if m else [])
        totals[m + 1].start(0, widen(jnp.concatenate(packed, axis=1)))
        swaps[1].wait()
        residual((1 - sub) * (blocks // 4))
        totals[m + 1].start(1, totals[m + 1].finish(0))
        packed = totals[m + 1].finish(1)
        cut = [packed[:, 16 * k : 16 * k + 16] for k in range(6)]
        row = lax.broadcasted_iota(jnp.int32, (16, 16), 0)
        col = lax.broadcasted_iota(jnp.int32, (16, 16), 1)
        eye = jnp.where(row == col, 1.0, 0.0).astype(F32)
        if m:
            rr, rq, rp, qq, qp, pp = cut
            lines = [[rr, rq, rp], [rq.T, qq, qp], [rp.T, qp.T, pp]]
        else:
            rr, rq, qq = cut[:3]
            lines = [[rr, rq], [rq.T, qq]]
        gram = jnp.concatenate([jnp.concatenate(line, axis=1) for line in lines], axis=0)
        alpha = qq - rq.T
        mix = [-eye, eye - alpha.T] + ([-coeffs[1]] if m else [])
        mix = jnp.concatenate(mix, axis=1)
        upper, inverse = factor(dot_t(dot(mix, gram), mix))
        coeffs[2 * m] = alpha
        coeffs[2 * m + 1] = upper
        following = dot(dot(inverse, mix), stack[...])
        if m:
            full[...] = following
            bases[1] = full[own_rows, :] * math.sqrt(nodes)
        else:
            second_stack[16:32] = following
            second_stack[32:48] = first_stack[16:32]
            bases[0] = second_stack[pl.ds(pl.multiple_of(16 + sub * 8, 8), 8), :] * math.sqrt(nodes)


def local(sizes, upper_tiles, tile_clusters, cluster_slot, start_block):
    nx, nz, ny = sizes
    blocks, cluster, _ = upper_tiles.shape
    groups = nx * nz * ny
    columns = blocks * cluster
    count = 2 * blocks
    targets = cluster_slot.at[tile_clusters].get(mode="promise_in_bounds").reshape(-1)
    owners = targets // blocks
    order = jnp.arange(count, dtype=jnp.int32)
    before = (owners[:, None] == owners[None, :]) & (order[None, :] < order[:, None])
    where = owners * CAP + jnp.sum(before.astype(jnp.int32), axis=1)
    taken = where[None, :] == jnp.arange(groups * CAP, dtype=jnp.int32)[:, None]
    placed = count - jnp.sum(jnp.where(taken, count - order[None, :], 0), axis=1)
    inside = targets % blocks
    out_ids = blocks - jnp.sum(jnp.where(taken, blocks - inside[None, :], 0), axis=1)
    out_ids = jnp.pad(out_ids.reshape(groups, 1, CAP), ((0, 0), (0, 0), (0, 128 - CAP)))
    names = jnp.concatenate([inside, jnp.full((1,), blocks, jnp.int32)])
    names = jnp.broadcast_to(names.astype(F32)[:, None], (count + 1, 128))

    dma = pltpu.SemaphoreType.DMA
    block = lambda n: pltpu.VMEM((n, 8, 128), F32)
    wide = lambda *shape: pltpu.VMEM(shape + (128,), F32)
    scratch = [
        pltpu.VMEM((16, columns), F32),
        pltpu.VMEM((32, columns), F32),
        pltpu.VMEM((48, columns), F32),
        block(count + 1),
        wide(groups, CAP),
        wide(groups, CAP),
        wide(blocks),
        wide(blocks),
        wide(blocks),
        wide(blocks),
        pltpu.VMEM((groups, 1, 128), jnp.int32),
        pltpu.SMEM((groups, 1, 128), jnp.int32),
        pltpu.VMEM((CAP, blocks, groups), BF16),
        block(blocks + 1),
        block(count + 1),
        pltpu.VMEM((groups, 16 * CAP, 128), BF16),
        pltpu.VMEM((2, groups, 16 * CAP, 128), BF16),
        block(groups * CAP),
        wide(groups * CAP * 8 + CAP * 8),
        wide(blocks * 8 + 8),
        wide(2, blocks * 8),
        wide(3, nx * ny, 16),
        wide(3, nz * 2, 16),
        dma((3, 2)),
        dma((3, 2)),
        dma,
        dma,
        dma,
        dma((6,)),
        dma((6,)),
        dma((2, CAP)),
        dma((2, CAP)),
        dma((2, CAP)),
        dma,
        dma,
        dma,
        dma,
    ]
    return pl.pallas_call(
        functools.partial(kernel, sizes, blocks, columns * groups),
        out_shape=[
            jax.ShapeDtypeStruct((2, 8, columns), F32),
            jax.ShapeDtypeStruct((4, 16, 16), F32),
        ],
        in_specs=[VMEM, VMEM, VMEM, VMEM, SMEM, SMEM],
        out_specs=[VMEM, VMEM],
        scratch_shapes=scratch,
        compiler_params=pltpu.CompilerParams(collective_id=1, has_side_effects=True, vmem_limit_bytes=LIMIT),
        name="lanczos",
    )(upper_tiles, start_block, names, out_ids, placed, where)


def solution(mesh):
    sizes = (4, 8, 4)
    in_specs = (P("rows", None, "sub"), P("rows", "sub"), P(), P("sub", "rows"))
    out_specs = (P(None, "sub", "rows"), P())
    body = functools.partial(local, sizes)
    return jax.shard_map(body, mesh=mesh, in_specs=in_specs, out_specs=out_specs, check_vma=False)
```

```python
import functools
import math

import jax
import jax.numpy as jnp
from jax import lax
from jax.experimental import pallas as pl
from jax.experimental.pallas import tpu as pltpu
from jax.sharding import PartitionSpec as P

CAP = 3
MESH = pl.DeviceIdType.MESH
VMEM = pl.BlockSpec(memory_space=pltpu.VMEM)
SMEM = pl.BlockSpec(memory_space=pltpu.SMEM)
F32 = jnp.float32
BF16 = jnp.bfloat16
LIMIT = 32 << 20
EXACT = lax.Precision.HIGHEST


def dot(left, right):
    return jnp.dot(left, right, precision=EXACT, preferred_element_type=F32)


def dot_t(left, right):
    dims = (((1,), (1,)), ((), ()))
    return lax.dot_general(left, right, dims, precision=EXACT, preferred_element_type=F32)


def swap(x):
    return pltpu.roll(x, 64, 1)


def is_low(shape):
    return lax.broadcasted_iota(jnp.int32, shape, 1) < 64


def pair_up(first, second):
    low = is_low(first.shape)
    return jnp.where(low, first, swap(second)), jnp.where(low, swap(first), second)


class Place:
    def __init__(self, sizes):
        self.nx, self.nz, self.ny = sizes
        self.groups = self.nx * self.nz * self.ny
        self.me, self.sub = lax.axis_index("rows"), lax.axis_index("sub")
        self.x = self.me // (self.nz * self.ny)
        self.z = lax.rem(self.me // self.ny, self.nz)
        self.y = lax.rem(self.me, self.ny)
        self.other = (self.me, 1 - self.sub)
        nx, nz, ny = sizes
        self.plane = [self.at(a, 0, b, 0) for a in range(nx) for b in range(ny)][1:]
        self.line = [self.at(0, a, 0, s) for a in range(nz) for s in range(2)][1:]
        self.slots = (self.x * ny + self.y, self.z * 2 + self.sub)

    def at(self, dx, dz, dy, ds):
        x, z, y = lax.rem(self.x + dx, self.nx), lax.rem(self.z + dz, self.nz), lax.rem(self.y + dy, self.ny)
        return ((x * self.nz + z) * self.ny + y, lax.rem(self.sub + ds, 2))

    def peer(self, i):
        return (lax.rem(self.me + i, self.groups), self.sub)


def signal(barrier, device):
    pl.semaphore_signal(barrier, inc=1, device_id=device, device_id_type=MESH)


def meet(place, everyone):
    barrier = pltpu.get_barrier_semaphore()
    if everyone:
        def greet(i, carry):
            signal(barrier, place.peer(i))
            return carry

        lax.fori_loop(1, place.groups, greet, 0, unroll=8)
        rest = [d for k, d in enumerate(place.line) if k % 2 == 0]
        count = place.groups - 1 + len(rest)
    else:
        rest = place.plane + place.line
        count = len(rest)
    for device in rest:
        signal(barrier, device)
    return lambda: pl.semaphore_wait(barrier, count)


def remote(src, dst, send_sem, recv_sem, device):
    return pltpu.make_async_remote_copy(
        src_ref=src, dst_ref=dst, send_sem=send_sem, recv_sem=recv_sem, device_id=device, device_id_type=MESH
    )


class Total:
    def __init__(self, place, near, far, send_sem, recv_sem):
        self.hops = ((near, place.slots[0], place.plane), (far, place.slots[1], place.line))
        self.sems = (send_sem, recv_sem)

    def copy(self, k, ref, device):
        return remote(ref, ref, self.sems[0].at[k], self.sems[1].at[k], device)

    def start(self, k, value):
        held, slot, peers = self.hops[k]
        held[pl.ds(slot, 1)] = value[None]
        for device in peers:
            self.copy(k, held.at[slot], device).start()

    def finish(self, k):
        held, _, peers = self.hops[k]
        self.copy(k, held.at[pl.ds(0, len(peers))], peers[0]).wait()
        return jnp.sum(held[...], axis=0)


class Exchange:
    def __init__(self, place, src, dst, send_sem, recv_sem, own_sem, rows=None):
        self.place, self.src, self.dst = place, src, dst
        self.sems, self.own_sem, self.rows = (send_sem, recv_sem), own_sem, rows

    def part(self, ref, i):
        return ref.at[i] if self.rows is None else ref.at[i, self.rows]

    def own(self):
        me = self.place.me
        return pltpu.make_async_copy(self.part(self.src, me), self.part(self.dst, me), self.own_sem)

    def start(self, build, unroll=2):
        place = self.place
        build(place.me)
        self.own().start()

        def send(i, carry):
            device = place.peer(i)
            build(device[0])
            remote(self.part(self.src, device[0]), self.part(self.dst, place.me), *self.sems, device).start()
            return carry

        lax.fori_loop(1, place.groups, send, 0, unroll=unroll)

    def rest(self):
        rest = pl.ds(0, self.place.groups - 1)
        return remote(self.part(self.src, rest), self.part(self.dst, rest), *self.sems, self.place.peer(1))

    def receive(self):
        self.own().wait()
        self.rest().wait_recv()

    def sent(self):
        self.rest().wait_send()

def factor(gram):
    n = gram.shape[0]
    row = lax.broadcasted_iota(jnp.int32, (n, n), 0)
    col = lax.broadcasted_iota(jnp.int32, (n, n), 1)
    left = gram
    right = jnp.where(row == col, 1.0, 0.0).astype(F32)
    below = lax.broadcasted_iota(jnp.int32, (n, 1), 0)
    for i in range(n):
        share = jnp.where(below > i, left[:, i : i + 1] / left[i : i + 1, i : i + 1], 0.0)
        right = right - share * right[i : i + 1, :]
        left = left - share * left[i : i + 1, :]
    pivots = jnp.sum(jnp.where(row == col, left, 0.0), axis=1, keepdims=True)
    root = lax.rsqrt(pivots)
    return jnp.where(col >= row, left * root, 0.0), right * root


def fold(x):
    width = x.shape[1]
    return jnp.concatenate([x[0:8], x[8:16], jnp.zeros((8, 128 - 2 * width), F32)], axis=1)


def unfold(x, width):
    return jnp.concatenate([x[:, :width], x[:, width : 2 * width]], axis=0)


def pieces(x):
    high = x.astype(BF16)
    rest = x - high.astype(F32)
    middle = rest.astype(BF16)
    return jnp.concatenate([high, middle, (rest - middle.astype(F32)).astype(BF16)], axis=0)


def gram_of(left, right):
    rows, width = left.shape[0], right.shape[0]
    dims = (((1,), (1,)), ((), ()))
    out = lax.dot_general(pieces(left), pieces(right), dims, preferred_element_type=F32)
    out = out[0:rows] + out[rows : 2 * rows] + out[2 * rows :]
    return out[:, :width] + out[:, width : 2 * width] + out[:, 2 * width :]


def kernel(
    sizes, blocks, nodes, tiles, start, names, placed, where, bases, coeffs,
    full, first_stack, second_stack, named, out_columns, in_columns, own_degree, degree, their_degree, scale,
    onehot, onehot_t, scaled, mirrored, reply, chunks, received, partners, returned, product, theirs,
    near, far, tsend, trecv, csend, crecv, cown, xsend, xrecv, asend, arecv, aown,
):
    place = Place(sizes)
    ready = meet(place, True)
    groups, sub = place.groups, place.sub
    columns = full.shape[1]
    half = columns // 2
    own_half = pl.ds(pl.multiple_of(sub * half, 128), half)
    own_rows = pl.ds(pl.multiple_of(sub * 8, 8), 8)
    totals = [Total(place, near.at[i], far.at[i], tsend.at[i], trecv.at[i]) for i in range(5)]

    def pair(i, src, dst):
        return remote(src, dst, xsend.at[i], xrecv.at[i], place.other)

    full[own_rows, :] = start[...]
    named[2 * blocks] = jnp.broadcast_to(names[pl.ds(2 * blocks, 1), :], (8, 128))
    mirrored[2 * blocks] = jnp.zeros((8, 128), F32)
    across = (((1,), (1,)), ((), ()))

    def sums(b, carry):
        tile = tiles[b]
        down = jnp.dot(jnp.ones((8, 64), BF16), tile, preferred_element_type=F32)
        low = is_low(down.shape)
        named[2 * b] = jnp.where(low, down, names[pl.ds(2 * b, 1), :])
        named[2 * b + 1] = jnp.where(low, swap(down), names[pl.ds(2 * b + 1, 1), :])
        along = lax.dot_general(jnp.ones((8, 128), BF16), tile, across, preferred_element_type=F32)
        own_degree[pl.ds(b, 1), :] = jnp.concatenate([along, along], axis=1)[0:1]
        return carry

    lax.fori_loop(0, blocks, sums, 0, unroll=4)

    ready()
    swap_rows = pair(0, start, full.at[own_rows])
    swap_rows.start()

    def fill(d, carry):
        for k in range(CAP):
            out_columns[d, pl.ds(k, 1), :] = named[placed[CAP * d + k]][0:1]
        return carry

    lax.fori_loop(0, groups, fill, 0, unroll=4)
    swap_rows.wait()
    totals[0].start(0, fold(gram_of(full[:, own_half], full[:, own_half])))
    sent_columns = Exchange(place, out_columns, in_columns, csend, crecv, cown)
    sent_columns.start(lambda d: None, unroll=4)
    totals[0].start(1, totals[0].finish(0))

    sent_columns.receive()
    sums_in = jnp.zeros((blocks, 128), F32)
    for k in range(CAP):
        rows = in_columns[:, k, :]
        index = lax.broadcasted_iota(jnp.int32, (blocks, groups), 0).astype(F32)
        match = jnp.where(index == rows.T[64:65, :], 1.0, 0.0).astype(F32)
        index = lax.broadcasted_iota(jnp.int32, (groups, blocks), 1).astype(F32)
        onehot_t[k] = jnp.where(index == rows[:, 64:65], 1.0, 0.0).astype(BF16)
        onehot[k] = match.astype(BF16)
        sums_in = sums_in + dot(match, rows)
    degree[...] = own_degree[...] + jnp.where(is_low(sums_in.shape), sums_in, swap(sums_in))
    swap_degree = pair(1, degree, their_degree)
    swap_degree.start()
    sent_columns.sent()
    swap_degree.wait()
    scale[...] = lax.rsqrt(degree[...] + their_degree[...])
    _, inverse = factor(unfold(totals[0].finish(1), 16))
    first_stack[16:32] = dot(inverse, full[...])

    def scale_of(b):
        return jnp.broadcast_to(scale[pl.ds(b, 1), :], (8, 128))

    def block_rows(b):
        return pl.ds(pl.multiple_of(b * 8, 8), 8)

    for m, stack in enumerate((first_stack, second_stack)):
        def scale_blocks(t, carry):
            lanes = pl.ds(pl.multiple_of(t * 128, 128), 128)
            pairs = pair_up(stack[16:24, lanes], stack[24:32, lanes])
            for p in range(2):
                scaled[block_rows(2 * t + p), :] = pairs[p] * scale_of(2 * t + p)
            return carry

        lax.fori_loop(0, blocks // 2, scale_blocks, 0, unroll=4)

        def mirror(b, carry):
            block = scaled[block_rows(b), :]
            left = jnp.concatenate([block, swap(block)], axis=0)[:, :64].astype(BF16)
            out = jnp.dot(left, tiles[b], preferred_element_type=F32)
            mirrored[2 * b], mirrored[2 * b + 1] = pair_up(out[0:8], out[8:16])
            return carry

        def answer(slots):
            for j in range(8):
                rows = scaled[pl.ds(j, blocks, stride=8), :].astype(BF16)
                for k in slots:
                    chosen = jnp.dot(onehot_t[k], rows, preferred_element_type=F32)
                    reply[pl.ds(8 * k + j, groups, stride=24), :] = chosen

        def builder(k):
            def build(d):
                if k == 0:
                    value = reply[pl.ds(pl.multiple_of(24 * d, 8), 16), :]
                elif k == 1:
                    last = reply[pl.ds(pl.multiple_of(24 * d + 16, 8), 8), :]
                    value = jnp.concatenate([last, mirrored[placed[CAP * d]]], axis=0)
                else:
                    value = jnp.concatenate([mirrored[placed[CAP * d + s]] for s in (1, 2)], axis=0)
                chunks[d, pl.ds(16 * k, 16), :] = value.astype(BF16)

            return build

        parts = [
            Exchange(
                place, chunks, received.at[m], asend.at[m, k], arecv.at[m, k], aown.at[m, k], pl.ds(16 * k, 16)
            )
            for k in range(CAP)
        ]
        answer((0, 1))
        parts[0].start(builder(0), unroll=4)
        answer((2,))
        lax.fori_loop(0, blocks, mirror, 0, unroll=4)
        parts[1].start(builder(1))
        parts[2].start(builder(2))
        known = gram_of(stack[16:, own_half], stack[16:, own_half])
        if m:
            known = jnp.concatenate([known[0:16], known[16:32, 16:32]], axis=1)
        totals[3 + m].start(0, fold(known))

        parts[0].receive()
        parts[1].receive()

        def spread(d, carry):
            chunk = received[m, d, pl.ds(0, 32), :].astype(F32)
            for k in range(CAP):
                partners[d * CAP + k] = chunk[8 * k : 8 * k + 8]
            returned[pl.ds(pl.multiple_of(d * 24, 8), 8), :] = chunk[24:32]
            return carry

        lax.fori_loop(0, groups, spread, 0, unroll=4)

        def forward(b, carry):
            low, high = pair_up(partners[where[2 * b]], partners[where[2 * b + 1]])
            left = jnp.concatenate([low, high], axis=0).astype(BF16)
            out = lax.dot_general(left, tiles[b], across, preferred_element_type=F32)
            product[block_rows(b), :] = jnp.concatenate([out[0:8], out[8:16]], axis=1)
            return carry

        lax.fori_loop(0, blocks, forward, 0, unroll=4)
        parts[2].receive()

        def spread_last(d, carry):
            chunk = received[m, d, pl.ds(32, 16), :].astype(F32)
            returned[pl.ds(pl.multiple_of(d * 24 + 8, 8), 16), :] = chunk
            return carry

        lax.fori_loop(0, groups, spread_last, 0, unroll=4)
        for j in range(8):
            added = jnp.zeros((blocks, 128), F32)
            for k in range(CAP):
                rows = returned[pl.ds(8 * k + j, groups, stride=24), :].astype(BF16)
                added = added + jnp.dot(onehot[k], rows, preferred_element_type=F32)
            lines = pl.ds(j, blocks, stride=8)
            product[lines, :] = product[lines, :] + added

        height = blocks * 4
        halves = [pl.ds(pl.multiple_of(s * height, 8), height) for s in (1 - sub, sub)]
        swaps = [pair(2 + 2 * m + i, product.at[h], theirs.at[m, h]) for i, h in enumerate(halves)]
        for one in swaps:
            one.start()
        totals[m + 3].start(1, totals[m + 3].finish(0))
        for part in parts:
            part.sent()

        def residual(first):
            def step(t, carry):
                t = first + t
                lanes = pl.ds(pl.multiple_of(t * 128, 128), 128)
                both = []
                for p in range(2):
                    b = 2 * t + p
                    both.append((product[block_rows(b), :] + theirs[m, block_rows(b), :]) * scale_of(b))
                stack[0:8, lanes], stack[8:16, lanes] = pair_up(both[0], both[1])
                return carry

            lax.fori_loop(0, blocks // 4, step, 0, unroll=4)

        swaps[0].wait()
        residual(sub * (blocks // 4))
        totals[m + 1].start(0, fold(gram_of(stack[0:16, own_half], stack[:, own_half])))
        swaps[1].wait()
        residual((1 - sub) * (blocks // 4))
        totals[m + 1].start(1, totals[m + 1].finish(0))
        known = unfold(totals[m + 3].finish(1), 48 if m else 16)
        cross = unfold(totals[m + 1].finish(1), 48 if m else 32)
        cut = [x[:, 16 * k : 16 * k + 16] for x in (cross, known) for k in range(x.shape[1] // 16)]
        row = lax.broadcasted_iota(jnp.int32, (16, 16), 0)
        col = lax.broadcasted_iota(jnp.int32, (16, 16), 1)
        eye = jnp.where(row == col, 1.0, 0.0).astype(F32)
        if m:
            rr, rq, rp, qq, qp, pp = cut
            lines = [[rr, rq, rp], [rq.T, qq, qp], [rp.T, qp.T, pp]]
        else:
            rr, rq, qq = cut
            lines = [[rr, rq], [rq.T, qq]]
        gram = jnp.concatenate([jnp.concatenate(line, axis=1) for line in lines], axis=0)
        alpha = qq - rq.T
        mix = [-eye, eye - alpha.T] + ([-coeffs[1]] if m else [])
        mix = jnp.concatenate(mix, axis=1)
        upper, inverse = factor(dot_t(dot(mix, gram), mix))
        coeffs[2 * m] = alpha
        coeffs[2 * m + 1] = upper
        following = dot(dot(inverse, mix), stack[...])
        if m:
            full[...] = following
            bases[1] = full[own_rows, :] * math.sqrt(nodes)
        else:
            second_stack[16:32] = following
            second_stack[32:48] = first_stack[16:32]
            bases[0] = second_stack[pl.ds(pl.multiple_of(16 + sub * 8, 8), 8), :] * math.sqrt(nodes)


def local(sizes, upper_tiles, tile_clusters, cluster_slot, start_block):
    nx, nz, ny = sizes
    blocks, cluster, _ = upper_tiles.shape
    groups = nx * nz * ny
    columns = blocks * cluster
    count = 2 * blocks
    targets = cluster_slot.at[tile_clusters].get(mode="promise_in_bounds").reshape(-1)
    owners = targets // blocks
    order = jnp.arange(count, dtype=jnp.int32)
    before = (owners[:, None] == owners[None, :]) & (order[None, :] < order[:, None])
    where = owners * CAP + jnp.sum(before.astype(jnp.int32), axis=1)
    taken = where[None, :] == jnp.arange(groups * CAP, dtype=jnp.int32)[:, None]
    placed = count - jnp.sum(jnp.where(taken, count - order[None, :], 0), axis=1)
    inside = targets % blocks
    names = jnp.concatenate([inside, jnp.full((1,), blocks, jnp.int32)])
    names = jnp.broadcast_to(names.astype(F32)[:, None], (count + 1, 128))

    dma = pltpu.SemaphoreType.DMA
    block = lambda n: pltpu.VMEM((n, 8, 128), F32)
    wide = lambda *shape: pltpu.VMEM(shape + (128,), F32)
    scratch = [
        pltpu.VMEM((16, columns), F32),
        pltpu.VMEM((32, columns), F32),
        pltpu.VMEM((48, columns), F32),
        block(count + 1),
        wide(groups, CAP),
        wide(groups, CAP),
        wide(blocks),
        wide(blocks),
        wide(blocks),
        wide(blocks),
        pltpu.VMEM((CAP, blocks, groups), BF16),
        pltpu.VMEM((CAP, groups, blocks), BF16),
        wide(blocks * 8 + 8),
        block(count + 1),
        wide(groups * CAP * 8 + CAP * 8),
        pltpu.VMEM((groups, 16 * CAP, 128), BF16),
        pltpu.VMEM((2, groups, 16 * CAP, 128), BF16),
        block(groups * CAP),
        wide(groups * CAP * 8 + CAP * 8),
        wide(blocks * 8 + 8),
        wide(2, blocks * 8),
        wide(5, nx * ny, 8),
        wide(5, nz * 2, 8),
        dma((5, 2)),
        dma((5, 2)),
        dma,
        dma,
        dma,
        dma((6,)),
        dma((6,)),
        dma((2, CAP)),
        dma((2, CAP)),
        dma((2, CAP)),
    ]
    return pl.pallas_call(
        functools.partial(kernel, sizes, blocks, columns * groups),
        out_shape=[
            jax.ShapeDtypeStruct((2, 8, columns), F32),
            jax.ShapeDtypeStruct((4, 16, 16), F32),
        ],
        in_specs=[VMEM, VMEM, VMEM, SMEM, SMEM],
        out_specs=[VMEM, VMEM],
        scratch_shapes=scratch,
        compiler_params=pltpu.CompilerParams(collective_id=1, has_side_effects=True, vmem_limit_bytes=LIMIT),
        name="lanczos",
    )(upper_tiles, start_block, names, placed, where)


def solution(mesh):
    sizes = (4, 8, 4)
    in_specs = (P("rows", None, "sub"), P("rows", "sub"), P(), P("sub", "rows"))
    out_specs = (P(None, "sub", "rows"), P())
    body = functools.partial(local, sizes)
    return jax.shard_map(body, mesh=mesh, in_specs=in_specs, out_specs=out_specs, check_vma=False)
```

```python
import functools
import math

import jax
import jax.numpy as jnp
from jax import lax
from jax.experimental import pallas as pl
from jax.experimental.pallas import tpu as pltpu
from jax.sharding import PartitionSpec as P

CAP = 3
MESH = pl.DeviceIdType.MESH
VMEM = pl.BlockSpec(memory_space=pltpu.VMEM)
SMEM = pl.BlockSpec(memory_space=pltpu.SMEM)
F32 = jnp.float32
BF16 = jnp.bfloat16
LIMIT = 32 << 20
EXACT = lax.Precision.HIGHEST


def dot(left, right):
    return jnp.dot(left, right, precision=EXACT, preferred_element_type=F32)


def dot_t(left, right):
    dims = (((1,), (1,)), ((), ()))
    return lax.dot_general(left, right, dims, precision=EXACT, preferred_element_type=F32)


def swap(x):
    return pltpu.roll(x, 64, 1)


def is_low(shape):
    return lax.broadcasted_iota(jnp.int32, shape, 1) < 64


def pair_up(first, second):
    low = is_low(first.shape)
    return jnp.where(low, first, swap(second)), jnp.where(low, swap(first), second)


class Place:
    def __init__(self, sizes):
        self.nx, self.nz, self.ny = sizes
        self.groups = self.nx * self.nz * self.ny
        self.me, self.sub = lax.axis_index("rows"), lax.axis_index("sub")
        self.x = self.me // (self.nz * self.ny)
        self.z = lax.rem(self.me // self.ny, self.nz)
        self.y = lax.rem(self.me, self.ny)
        self.other = (self.me, 1 - self.sub)
        nx, nz, ny = sizes
        self.plane = [self.at(a, 0, b, 0) for a in range(nx) for b in range(ny)][1:]
        self.line = [self.at(0, a, 0, s) for a in range(nz) for s in range(2)][1:]
        self.slots = (self.x * ny + self.y, self.z * 2 + self.sub)

    def at(self, dx, dz, dy, ds):
        x, z, y = lax.rem(self.x + dx, self.nx), lax.rem(self.z + dz, self.nz), lax.rem(self.y + dy, self.ny)
        return ((x * self.nz + z) * self.ny + y, lax.rem(self.sub + ds, 2))

    def order(self):
        spans = [(0, self.nz // 2)] + [(self.nz // 2 - g, self.nz // 2 + g) for g in range(1, self.nz // 2)]
        wide = 2 * self.nx * self.ny
        for g, (one, two) in enumerate(spans):
            def peer(i, one=one, two=two):
                dz = one + (two - one) * lax.rem(i, 2)
                return self.at(i // (2 * self.ny), dz, lax.rem(i // 2, self.ny), 0)

            yield (1 if g == 0 else 0), wide, peer

    def peer(self, i):
        return (lax.rem(self.me + i, self.groups), self.sub)


def signal(barrier, device):
    pl.semaphore_signal(barrier, inc=1, device_id=device, device_id_type=MESH)


def meet(place, everyone):
    barrier = pltpu.get_barrier_semaphore()
    if everyone:
        def greet(i, carry):
            signal(barrier, place.peer(i))
            return carry

        lax.fori_loop(1, place.groups, greet, 0, unroll=8)
        rest = [d for k, d in enumerate(place.line) if k % 2 == 0]
        count = place.groups - 1 + len(rest)
    else:
        rest = place.plane + place.line
        count = len(rest)
    for device in rest:
        signal(barrier, device)
    return lambda: pl.semaphore_wait(barrier, count)


def remote(src, dst, send_sem, recv_sem, device):
    return pltpu.make_async_remote_copy(
        src_ref=src, dst_ref=dst, send_sem=send_sem, recv_sem=recv_sem, device_id=device, device_id_type=MESH
    )


class Total:
    def __init__(self, place, near, far, send_sem, recv_sem):
        self.hops = ((near, place.slots[0], place.plane), (far, place.slots[1], place.line))
        self.sems = (send_sem, recv_sem)

    def copy(self, k, ref, device):
        return remote(ref, ref, self.sems[0].at[k], self.sems[1].at[k], device)

    def start(self, k, value):
        held, slot, peers = self.hops[k]
        held[pl.ds(slot, 1)] = value[None]
        for device in peers:
            self.copy(k, held.at[slot], device).start()

    def finish(self, k):
        held, _, peers = self.hops[k]
        self.copy(k, held.at[pl.ds(0, len(peers))], peers[0]).wait()
        return jnp.sum(held[...], axis=0)


class Exchange:
    def __init__(self, place, src, dst, send_sem, recv_sem, own_sem, rows=None):
        self.place, self.src, self.dst = place, src, dst
        self.sems, self.own_sem, self.rows = (send_sem, recv_sem), own_sem, rows

    def part(self, ref, i):
        return ref.at[i] if self.rows is None else ref.at[i, self.rows]

    def own(self):
        me = self.place.me
        return pltpu.make_async_copy(self.part(self.src, me), self.part(self.dst, me), self.own_sem)

    def start(self, build, unroll=2):
        place = self.place
        build(place.me)
        self.own().start()
        for begin, end, peer in place.order():
            def send(i, carry):
                device = peer(i)
                build(device[0])
                remote(self.part(self.src, device[0]), self.part(self.dst, place.me), *self.sems, device).start()
                return carry

            lax.fori_loop(begin, end, send, 0, unroll=unroll)

    def rest(self):
        rest = pl.ds(0, self.place.groups - 1)
        return remote(self.part(self.src, rest), self.part(self.dst, rest), *self.sems, self.place.peer(1))

    def receive(self):
        self.own().wait()
        self.rest().wait_recv()

    def sent(self):
        self.rest().wait_send()

def factor(gram):
    n = gram.shape[0]
    row = lax.broadcasted_iota(jnp.int32, (n, n), 0)
    col = lax.broadcasted_iota(jnp.int32, (n, n), 1)
    left = gram
    right = jnp.where(row == col, 1.0, 0.0).astype(F32)
    below = lax.broadcasted_iota(jnp.int32, (n, 1), 0)
    for i in range(n):
        share = jnp.where(below > i, left[:, i : i + 1] / left[i : i + 1, i : i + 1], 0.0)
        right = right - share * right[i : i + 1, :]
        left = left - share * left[i : i + 1, :]
    pivots = jnp.sum(jnp.where(row == col, left, 0.0), axis=1, keepdims=True)
    root = lax.rsqrt(pivots)
    return jnp.where(col >= row, left * root, 0.0), right * root


def fold(x):
    width = x.shape[1]
    return jnp.concatenate([x[0:8], x[8:16], jnp.zeros((8, 128 - 2 * width), F32)], axis=1)


def unfold(x, width):
    return jnp.concatenate([x[:, :width], x[:, width : 2 * width]], axis=0)


def pieces(x):
    high = x.astype(BF16)
    rest = x - high.astype(F32)
    middle = rest.astype(BF16)
    return jnp.concatenate([high, middle, (rest - middle.astype(F32)).astype(BF16)], axis=0)


def gram_of(left, right):
    rows, width = left.shape[0], right.shape[0]
    dims = (((1,), (1,)), ((), ()))
    out = lax.dot_general(pieces(left), pieces(right), dims, preferred_element_type=F32)
    out = out[0:rows] + out[rows : 2 * rows] + out[2 * rows :]
    return out[:, :width] + out[:, width : 2 * width] + out[:, 2 * width :]


def kernel(
    sizes, blocks, nodes, tiles, start, their_start, names, placed, where, bases, coeffs,
    full, first_stack, second_stack, named, out_columns, in_columns, own_degree, degree, their_degree, scale,
    onehot, onehot_t, scaled, mirrored, reply, chunks, received, partners, returned, product, theirs,
    near, far, tsend, trecv, csend, crecv, cown, xsend, xrecv, asend, arecv, aown,
):
    place = Place(sizes)
    ready = meet(place, True)
    groups, sub = place.groups, place.sub
    columns = full.shape[1]
    half = columns // 2
    own_half = pl.ds(pl.multiple_of(sub * half, 128), half)
    own_rows = pl.ds(pl.multiple_of(sub * 8, 8), 8)
    totals = [Total(place, near.at[i], far.at[i], tsend.at[i], trecv.at[i]) for i in range(5)]

    def pair(i, src, dst):
        return remote(src, dst, xsend.at[i], xrecv.at[i], place.other)

    full[own_rows, :] = start[...]
    full[pl.ds(pl.multiple_of(8 - sub * 8, 8), 8), :] = their_start[...]
    named[2 * blocks] = jnp.broadcast_to(names[pl.ds(2 * blocks, 1), :], (8, 128))
    mirrored[2 * blocks] = jnp.zeros((8, 128), F32)
    across = (((1,), (1,)), ((), ()))

    def sums(b, carry):
        tile = tiles[b]
        down = jnp.dot(jnp.ones((8, 64), BF16), tile, preferred_element_type=F32)
        low = is_low(down.shape)
        named[2 * b] = jnp.where(low, down, names[pl.ds(2 * b, 1), :])
        named[2 * b + 1] = jnp.where(low, swap(down), names[pl.ds(2 * b + 1, 1), :])
        along = lax.dot_general(jnp.ones((8, 128), BF16), tile, across, preferred_element_type=F32)
        own_degree[pl.ds(b, 1), :] = jnp.concatenate([along, along], axis=1)[0:1]
        return carry

    lax.fori_loop(0, blocks, sums, 0, unroll=4)

    first = fold(gram_of(full[:, own_half], full[:, own_half]))
    ready()
    totals[0].start(0, first)

    def fill(d):
        for k in range(CAP):
            out_columns[d, pl.ds(k, 1), :] = named[placed[CAP * d + k]][0:1]

    sent_columns = Exchange(place, out_columns, in_columns, csend, crecv, cown)
    sent_columns.start(fill, unroll=4)
    totals[0].start(1, totals[0].finish(0))

    sent_columns.receive()
    sums_in = jnp.zeros((blocks, 128), F32)
    for k in range(CAP):
        rows = in_columns[:, k, :]
        index = lax.broadcasted_iota(jnp.int32, (blocks, groups), 0).astype(F32)
        match = jnp.where(index == rows.T[64:65, :], 1.0, 0.0).astype(F32)
        index = lax.broadcasted_iota(jnp.int32, (groups, blocks), 1).astype(F32)
        onehot_t[k] = jnp.where(index == rows[:, 64:65], 1.0, 0.0).astype(BF16)
        onehot[k] = match.astype(BF16)
        sums_in = sums_in + dot(match, rows)
    degree[...] = own_degree[...] + jnp.where(is_low(sums_in.shape), sums_in, swap(sums_in))
    swap_degree = pair(1, degree, their_degree)
    swap_degree.start()
    sent_columns.sent()
    swap_degree.wait()
    scale[...] = lax.rsqrt(degree[...] + their_degree[...])
    _, inverse = factor(unfold(totals[0].finish(1), 16))
    first_stack[16:32] = dot(inverse, full[...])

    def scale_of(b):
        return jnp.broadcast_to(scale[pl.ds(b, 1), :], (8, 128))

    def block_rows(b):
        return pl.ds(pl.multiple_of(b * 8, 8), 8)

    for m, stack in enumerate((first_stack, second_stack)):
        def scale_blocks(t, carry):
            lanes = pl.ds(pl.multiple_of(t * 128, 128), 128)
            pairs = pair_up(stack[16:24, lanes], stack[24:32, lanes])
            for p in range(2):
                scaled[block_rows(2 * t + p), :] = pairs[p] * scale_of(2 * t + p)
            return carry

        lax.fori_loop(0, blocks // 2, scale_blocks, 0, unroll=4)

        def mirror(b, carry):
            block = scaled[block_rows(b), :]
            left = jnp.concatenate([block, swap(block)], axis=0)[:, :64].astype(BF16)
            out = jnp.dot(left, tiles[b], preferred_element_type=F32)
            mirrored[2 * b], mirrored[2 * b + 1] = pair_up(out[0:8], out[8:16])
            return carry

        def answer(slots):
            for j in range(8):
                rows = scaled[pl.ds(j, blocks, stride=8), :].astype(BF16)
                for k in slots:
                    chosen = jnp.dot(onehot_t[k], rows, preferred_element_type=F32)
                    reply[pl.ds(8 * k + j, groups, stride=24), :] = chosen

        def builder(k):
            def build(d):
                if k == 0:
                    value = reply[pl.ds(pl.multiple_of(24 * d, 8), 16), :]
                elif k == 1:
                    last = reply[pl.ds(pl.multiple_of(24 * d + 16, 8), 8), :]
                    value = jnp.concatenate([last, mirrored[placed[CAP * d]]], axis=0)
                else:
                    value = jnp.concatenate([mirrored[placed[CAP * d + s]] for s in (1, 2)], axis=0)
                chunks[d, pl.ds(16 * k, 16), :] = value.astype(BF16)

            return build

        parts = [
            Exchange(
                place, chunks, received.at[m], asend.at[m, k], arecv.at[m, k], aown.at[m, k], pl.ds(16 * k, 16)
            )
            for k in range(CAP)
        ]
        answer((0, 1))
        parts[0].start(builder(0), unroll=4)
        answer((2,))
        lax.fori_loop(0, blocks, mirror, 0, unroll=4)
        parts[1].start(builder(1))
        parts[2].start(builder(2))
        known = gram_of(stack[16:, own_half], stack[16:, own_half])
        if m:
            known = jnp.concatenate([known[0:16], known[16:32, 16:32]], axis=1)
        totals[3 + m].start(0, fold(known))

        parts[0].receive()
        parts[1].receive()

        def spread(d, carry):
            chunk = received[m, d, pl.ds(0, 32), :].astype(F32)
            for k in range(CAP):
                partners[d * CAP + k] = chunk[8 * k : 8 * k + 8]
            returned[pl.ds(pl.multiple_of(d * 24, 8), 8), :] = chunk[24:32]
            return carry

        lax.fori_loop(0, groups, spread, 0, unroll=4)

        def forward(b, carry):
            low, high = pair_up(partners[where[2 * b]], partners[where[2 * b + 1]])
            left = jnp.concatenate([low, high], axis=0).astype(BF16)
            out = lax.dot_general(left, tiles[b], across, preferred_element_type=F32)
            product[block_rows(b), :] = jnp.concatenate([out[0:8], out[8:16]], axis=1)
            return carry

        lax.fori_loop(0, blocks, forward, 0, unroll=4)
        parts[2].receive()

        def spread_last(d, carry):
            chunk = received[m, d, pl.ds(32, 16), :].astype(F32)
            returned[pl.ds(pl.multiple_of(d * 24 + 8, 8), 16), :] = chunk
            return carry

        lax.fori_loop(0, groups, spread_last, 0, unroll=4)
        for j in range(8):
            added = jnp.zeros((blocks, 128), F32)
            for k in range(CAP):
                rows = returned[pl.ds(8 * k + j, groups, stride=24), :].astype(BF16)
                added = added + jnp.dot(onehot[k], rows, preferred_element_type=F32)
            lines = pl.ds(j, blocks, stride=8)
            product[lines, :] = product[lines, :] + added

        height = blocks * 4
        halves = [pl.ds(pl.multiple_of(s * height, 8), height) for s in (1 - sub, sub)]
        swaps = [pair(2 + 2 * m + i, product.at[h], theirs.at[m, h]) for i, h in enumerate(halves)]
        for one in swaps:
            one.start()
        totals[m + 3].start(1, totals[m + 3].finish(0))
        for part in parts:
            part.sent()

        def residual(first):
            def step(t, carry):
                t = first + t
                lanes = pl.ds(pl.multiple_of(t * 128, 128), 128)
                both = []
                for p in range(2):
                    b = 2 * t + p
                    both.append((product[block_rows(b), :] + theirs[m, block_rows(b), :]) * scale_of(b))
                stack[0:8, lanes], stack[8:16, lanes] = pair_up(both[0], both[1])
                return carry

            lax.fori_loop(0, blocks // 4, step, 0, unroll=4)

        swaps[0].wait()
        residual(sub * (blocks // 4))
        totals[m + 1].start(0, fold(gram_of(stack[0:16, own_half], stack[:, own_half])))
        swaps[1].wait()
        residual((1 - sub) * (blocks // 4))
        totals[m + 1].start(1, totals[m + 1].finish(0))
        known = unfold(totals[m + 3].finish(1), 48 if m else 16)
        cross = unfold(totals[m + 1].finish(1), 48 if m else 32)
        cut = [x[:, 16 * k : 16 * k + 16] for x in (cross, known) for k in range(x.shape[1] // 16)]
        row = lax.broadcasted_iota(jnp.int32, (16, 16), 0)
        col = lax.broadcasted_iota(jnp.int32, (16, 16), 1)
        eye = jnp.where(row == col, 1.0, 0.0).astype(F32)
        if m:
            rr, rq, rp, qq, qp, pp = cut
            lines = [[rr, rq, rp], [rq.T, qq, qp], [rp.T, qp.T, pp]]
        else:
            rr, rq, qq = cut
            lines = [[rr, rq], [rq.T, qq]]
        gram = jnp.concatenate([jnp.concatenate(line, axis=1) for line in lines], axis=0)
        alpha = qq - rq.T
        mix = [-eye, eye - alpha.T] + ([-coeffs[1]] if m else [])
        mix = jnp.concatenate(mix, axis=1)
        upper, inverse = factor(dot_t(dot(mix, gram), mix))
        coeffs[2 * m] = alpha
        coeffs[2 * m + 1] = upper
        following = dot(dot(inverse, mix), stack[...])
        if m:
            full[...] = following
            bases[1] = full[own_rows, :] * math.sqrt(nodes)
        else:
            second_stack[16:32] = following
            second_stack[32:48] = first_stack[16:32]
            bases[0] = second_stack[pl.ds(pl.multiple_of(16 + sub * 8, 8), 8), :] * math.sqrt(nodes)


def local(sizes, upper_tiles, tile_clusters, cluster_slot, start_block):
    nx, nz, ny = sizes
    blocks, cluster, _ = upper_tiles.shape
    groups = nx * nz * ny
    columns = blocks * cluster
    count = 2 * blocks
    their_start = lax.ppermute(start_block, "sub", [(0, 1), (1, 0)])
    targets = cluster_slot.at[tile_clusters].get(mode="promise_in_bounds").reshape(-1)
    owners = targets // blocks
    order = jnp.arange(count, dtype=jnp.int32)
    before = (owners[:, None] == owners[None, :]) & (order[None, :] < order[:, None])
    where = owners * CAP + jnp.sum(before.astype(jnp.int32), axis=1)
    taken = where[None, :] == jnp.arange(groups * CAP, dtype=jnp.int32)[:, None]
    placed = count - jnp.sum(jnp.where(taken, count - order[None, :], 0), axis=1)
    inside = targets % blocks
    names = jnp.concatenate([inside, jnp.full((1,), blocks, jnp.int32)])
    names = jnp.broadcast_to(names.astype(F32)[:, None], (count + 1, 128))

    dma = pltpu.SemaphoreType.DMA
    block = lambda n: pltpu.VMEM((n, 8, 128), F32)
    wide = lambda *shape: pltpu.VMEM(shape + (128,), F32)
    scratch = [
        pltpu.VMEM((16, columns), F32),
        pltpu.VMEM((32, columns), F32),
        pltpu.VMEM((48, columns), F32),
        block(count + 1),
        wide(groups, CAP),
        wide(groups, CAP),
        wide(blocks),
        wide(blocks),
        wide(blocks),
        wide(blocks),
        pltpu.VMEM((CAP, blocks, groups), BF16),
        pltpu.VMEM((CAP, groups, blocks), BF16),
        wide(blocks * 8 + 8),
        block(count + 1),
        wide(groups * CAP * 8 + CAP * 8),
        pltpu.VMEM((groups, 16 * CAP, 128), BF16),
        pltpu.VMEM((2, groups, 16 * CAP, 128), BF16),
        block(groups * CAP),
        wide(groups * CAP * 8 + CAP * 8),
        wide(blocks * 8 + 8),
        wide(2, blocks * 8),
        wide(5, nx * ny, 8),
        wide(5, nz * 2, 8),
        dma((5, 2)),
        dma((5, 2)),
        dma,
        dma,
        dma,
        dma((6,)),
        dma((6,)),
        dma((2, CAP)),
        dma((2, CAP)),
        dma((2, CAP)),
    ]
    return pl.pallas_call(
        functools.partial(kernel, sizes, blocks, columns * groups),
        out_shape=[
            jax.ShapeDtypeStruct((2, 8, columns), F32),
            jax.ShapeDtypeStruct((4, 16, 16), F32),
        ],
        in_specs=[VMEM, VMEM, VMEM, VMEM, SMEM, SMEM],
        out_specs=[VMEM, VMEM],
        scratch_shapes=scratch,
        compiler_params=pltpu.CompilerParams(collective_id=1, has_side_effects=True, vmem_limit_bytes=LIMIT),
        name="lanczos",
    )(upper_tiles, start_block, their_start, names, placed, where)


def solution(mesh):
    sizes = (4, 8, 4)
    in_specs = (P("rows", None, "sub"), P("rows", "sub"), P(), P("sub", "rows"))
    out_specs = (P(None, "sub", "rows"), P())
    body = functools.partial(local, sizes)
    return jax.shard_map(body, mesh=mesh, in_specs=in_specs, out_specs=out_specs, check_vma=False)
```

```python
import functools
import math

import jax
import jax.numpy as jnp
from jax import lax
from jax.experimental import pallas as pl
from jax.experimental.pallas import tpu as pltpu
from jax.sharding import PartitionSpec as P

CAP = 3
MESH = pl.DeviceIdType.MESH
VMEM = pl.BlockSpec(memory_space=pltpu.VMEM)
SMEM = pl.BlockSpec(memory_space=pltpu.SMEM)
F32 = jnp.float32
BF16 = jnp.bfloat16
LIMIT = 32 << 20
EXACT = lax.Precision.HIGHEST


def dot(left, right):
    return jnp.dot(left, right, precision=EXACT, preferred_element_type=F32)


def dot_t(left, right):
    dims = (((1,), (1,)), ((), ()))
    return lax.dot_general(left, right, dims, precision=EXACT, preferred_element_type=F32)


def swap(x):
    return pltpu.roll(x, 64, 1)


def is_low(shape):
    return lax.broadcasted_iota(jnp.int32, shape, 1) < 64


def pair_up(first, second):
    low = is_low(first.shape)
    return jnp.where(low, first, swap(second)), jnp.where(low, swap(first), second)


class Place:
    def __init__(self, sizes):
        self.nx, self.nz, self.ny = sizes
        self.groups = self.nx * self.nz * self.ny
        self.me, self.sub = lax.axis_index("rows"), lax.axis_index("sub")
        self.x = self.me // (self.nz * self.ny)
        self.z = lax.rem(self.me // self.ny, self.nz)
        self.y = lax.rem(self.me, self.ny)
        self.other = (self.me, 1 - self.sub)
        nx, nz, ny = sizes
        self.plane = [self.at(a, 0, b, 0) for a in range(nx) for b in range(ny)][1:]
        self.line = [self.at(0, a, 0, s) for a in range(nz) for s in range(2)][1:]
        self.slots = (self.x * ny + self.y, self.z * 2 + self.sub)

    def at(self, dx, dz, dy, ds):
        x, z, y = lax.rem(self.x + dx, self.nx), lax.rem(self.z + dz, self.nz), lax.rem(self.y + dy, self.ny)
        return ((x * self.nz + z) * self.ny + y, lax.rem(self.sub + ds, 2))

    def order(self):
        spans = [(0, self.nz // 2)] + [(self.nz // 2 - g, self.nz // 2 + g) for g in range(1, self.nz // 2)]
        wide = 2 * self.nx * self.ny
        for g, (one, two) in enumerate(spans):
            def peer(i, one=one, two=two):
                dz = one + (two - one) * lax.rem(i, 2)
                return self.at(i // (2 * self.ny), dz, lax.rem(i // 2, self.ny), 0)

            yield (1 if g == 0 else 0), wide, peer

    def peer(self, i):
        return (lax.rem(self.me + i, self.groups), self.sub)


def signal(barrier, device):
    pl.semaphore_signal(barrier, inc=1, device_id=device, device_id_type=MESH)


def meet(place, everyone):
    barrier = pltpu.get_barrier_semaphore()
    if everyone:
        def greet(i, carry):
            signal(barrier, place.peer(i))
            return carry

        lax.fori_loop(1, place.groups, greet, 0, unroll=8)
        rest = [d for k, d in enumerate(place.line) if k % 2 == 0]
        count = place.groups - 1 + len(rest)
    else:
        rest = place.plane + place.line
        count = len(rest)
    for device in rest:
        signal(barrier, device)
    return lambda: pl.semaphore_wait(barrier, count)


def remote(src, dst, send_sem, recv_sem, device):
    return pltpu.make_async_remote_copy(
        src_ref=src, dst_ref=dst, send_sem=send_sem, recv_sem=recv_sem, device_id=device, device_id_type=MESH
    )


class Total:
    def __init__(self, place, near, far, send_sem, recv_sem):
        self.hops = ((near, place.slots[0], place.plane), (far, place.slots[1], place.line))
        self.sems = (send_sem, recv_sem)

    def copy(self, k, ref, device):
        return remote(ref, ref, self.sems[0].at[k], self.sems[1].at[k], device)

    def start(self, k, value):
        held, slot, peers = self.hops[k]
        held[pl.ds(slot, 1)] = value[None]
        for device in peers:
            self.copy(k, held.at[slot], device).start()

    def finish(self, k):
        held, _, peers = self.hops[k]
        self.copy(k, held.at[pl.ds(0, len(peers))], peers[0]).wait()
        return jnp.sum(held[...], axis=0)


class Exchange:
    def __init__(self, place, src, dst, send_sem, recv_sem, own_sem, rows=None):
        self.place, self.src, self.dst = place, src, dst
        self.sems, self.own_sem, self.rows = (send_sem, recv_sem), own_sem, rows

    def part(self, ref, i):
        return ref.at[i] if self.rows is None else ref.at[i, self.rows]

    def own(self):
        me = self.place.me
        return pltpu.make_async_copy(self.part(self.src, me), self.part(self.dst, me), self.own_sem)

    def start(self, build, unroll=2):
        place = self.place
        build(place.me)
        self.own().start()
        for begin, end, peer in place.order():
            def send(i, carry):
                device = peer(i)
                build(device[0])
                remote(self.part(self.src, device[0]), self.part(self.dst, place.me), *self.sems, device).start()
                return carry

            lax.fori_loop(begin, end, send, 0, unroll=unroll)

    def rest(self):
        rest = pl.ds(0, self.place.groups - 1)
        return remote(self.part(self.src, rest), self.part(self.dst, rest), *self.sems, self.place.peer(1))

    def receive(self):
        self.own().wait()
        self.rest().wait_recv()

    def sent(self):
        self.rest().wait_send()

def factor(gram):
    n = gram.shape[0]
    row = lax.broadcasted_iota(jnp.int32, (n, n), 0)
    col = lax.broadcasted_iota(jnp.int32, (n, n), 1)
    left = gram
    right = jnp.where(row == col, 1.0, 0.0).astype(F32)
    below = lax.broadcasted_iota(jnp.int32, (n, 1), 0)
    for i in range(n):
        share = jnp.where(below > i, left[:, i : i + 1] / left[i : i + 1, i : i + 1], 0.0)
        right = right - share * right[i : i + 1, :]
        left = left - share * left[i : i + 1, :]
    pivots = jnp.sum(jnp.where(row == col, left, 0.0), axis=1, keepdims=True)
    root = lax.rsqrt(pivots)
    return jnp.where(col >= row, left * root, 0.0), right * root


def fold(x):
    width = x.shape[1]
    return jnp.concatenate([x[0:8], x[8:16], jnp.zeros((8, 128 - 2 * width), F32)], axis=1)


def unfold(x, width):
    return jnp.concatenate([x[:, :width], x[:, width : 2 * width]], axis=0)


def beside(lines):
    return jnp.concatenate([jnp.concatenate(line, axis=1) for line in lines], axis=0)


def pieces(x):
    high = x.astype(BF16)
    rest = x - high.astype(F32)
    middle = rest.astype(BF16)
    return jnp.concatenate([high, middle, (rest - middle.astype(F32)).astype(BF16)], axis=0)


def gram_of(left, right):
    rows, width = left.shape[0], right.shape[0]
    dims = (((1,), (1,)), ((), ()))
    out = lax.dot_general(pieces(left), pieces(right), dims, preferred_element_type=F32)
    out = out[0:rows] + out[rows : 2 * rows] + out[2 * rows :]
    return out[:, :width] + out[:, width : 2 * width] + out[:, 2 * width :]


def kernel(
    sizes, blocks, nodes, tiles, start, their_start, names, placed, where, bases, coeffs,
    full, first_stack, second_stack, named, out_columns, in_columns, own_degree, degree, their_degree, scale,
    onehot, onehot_t, scaled, mirrored, reply, chunks, received, partners, returned, product, theirs,
    near, far, tsend, trecv, csend, crecv, cown, xsend, xrecv, asend, arecv, aown,
):
    place = Place(sizes)
    ready = meet(place, True)
    groups, sub = place.groups, place.sub
    columns = full.shape[1]
    half = columns // 2
    own_half = pl.ds(pl.multiple_of(sub * half, 128), half)
    own_rows = pl.ds(pl.multiple_of(sub * 8, 8), 8)
    totals = [Total(place, near.at[i], far.at[i], tsend.at[i], trecv.at[i]) for i in range(4)]

    def pair(i, src, dst):
        return remote(src, dst, xsend.at[i], xrecv.at[i], place.other)

    full[own_rows, :] = start[...]
    full[pl.ds(pl.multiple_of(8 - sub * 8, 8), 8), :] = their_start[...]
    named[2 * blocks] = jnp.broadcast_to(names[pl.ds(2 * blocks, 1), :], (8, 128))
    mirrored[2 * blocks] = jnp.zeros((8, 128), F32)
    across = (((1,), (1,)), ((), ()))

    def sums(b, carry):
        tile = tiles[b]
        down = jnp.dot(jnp.ones((8, 64), BF16), tile, preferred_element_type=F32)
        low = is_low(down.shape)
        named[2 * b] = jnp.where(low, down, names[pl.ds(2 * b, 1), :])
        named[2 * b + 1] = jnp.where(low, swap(down), names[pl.ds(2 * b + 1, 1), :])
        along = lax.dot_general(jnp.ones((8, 128), BF16), tile, across, preferred_element_type=F32)
        own_degree[pl.ds(b, 1), :] = jnp.concatenate([along, along], axis=1)[0:1]
        return carry

    lax.fori_loop(0, blocks, sums, 0, unroll=4)

    first = fold(gram_of(full[:, own_half], full[:, own_half]))
    ready()
    totals[0].start(0, first)

    def fill(d):
        for k in range(CAP):
            out_columns[d, pl.ds(k, 1), :] = named[placed[CAP * d + k]][0:1]

    sent_columns = Exchange(place, out_columns, in_columns, csend, crecv, cown)
    sent_columns.start(fill, unroll=4)
    totals[0].start(1, totals[0].finish(0))

    sent_columns.receive()
    sums_in = jnp.zeros((blocks, 128), F32)
    for k in range(CAP):
        rows = in_columns[:, k, :]
        index = lax.broadcasted_iota(jnp.int32, (blocks, groups), 0).astype(F32)
        match = jnp.where(index == rows.T[64:65, :], 1.0, 0.0).astype(F32)
        index = lax.broadcasted_iota(jnp.int32, (groups, blocks), 1).astype(F32)
        onehot_t[k] = jnp.where(index == rows[:, 64:65], 1.0, 0.0).astype(BF16)
        onehot[k] = match.astype(BF16)
        sums_in = sums_in + dot(match, rows)
    degree[...] = own_degree[...] + jnp.where(is_low(sums_in.shape), sums_in, swap(sums_in))
    swap_degree = pair(1, degree, their_degree)
    swap_degree.start()
    sent_columns.sent()
    swap_degree.wait()
    scale[...] = lax.rsqrt(degree[...] + their_degree[...])
    _, inverse = factor(unfold(totals[0].finish(1), 16))
    first_stack[16:32] = dot(inverse, full[...])

    def scale_of(b):
        return jnp.broadcast_to(scale[pl.ds(b, 1), :], (8, 128))

    def block_rows(b):
        return pl.ds(pl.multiple_of(b * 8, 8), 8)

    for m, stack in enumerate((first_stack, second_stack)):
        def scale_blocks(t, carry):
            lanes = pl.ds(pl.multiple_of(t * 128, 128), 128)
            pairs = pair_up(stack[16:24, lanes], stack[24:32, lanes])
            for p in range(2):
                scaled[block_rows(2 * t + p), :] = pairs[p] * scale_of(2 * t + p)
            return carry

        lax.fori_loop(0, blocks // 2, scale_blocks, 0, unroll=4)

        def mirror(b, carry):
            block = scaled[block_rows(b), :]
            left = jnp.concatenate([block, swap(block)], axis=0)[:, :64].astype(BF16)
            out = jnp.dot(left, tiles[b], preferred_element_type=F32)
            mirrored[2 * b], mirrored[2 * b + 1] = pair_up(out[0:8], out[8:16])
            return carry

        def answer(slots):
            for j in range(8):
                rows = scaled[pl.ds(j, blocks, stride=8), :].astype(BF16)
                for k in slots:
                    chosen = jnp.dot(onehot_t[k], rows, preferred_element_type=F32)
                    reply[pl.ds(8 * k + j, groups, stride=24), :] = chosen

        def builder(k):
            def build(d):
                if k == 0:
                    value = reply[pl.ds(pl.multiple_of(24 * d, 8), 16), :]
                elif k == 1:
                    last = reply[pl.ds(pl.multiple_of(24 * d + 16, 8), 8), :]
                    value = jnp.concatenate([last, mirrored[placed[CAP * d]]], axis=0)
                else:
                    value = jnp.concatenate([mirrored[placed[CAP * d + s]] for s in (1, 2)], axis=0)
                chunks[d, pl.ds(16 * k, 16), :] = value.astype(BF16)

            return build

        parts = [
            Exchange(
                place, chunks, received.at[m], asend.at[m, k], arecv.at[m, k], aown.at[m, k], pl.ds(16 * k, 16)
            )
            for k in range(CAP)
        ]
        answer((0, 1))
        parts[0].start(builder(0), unroll=4)
        answer((2,))
        lax.fori_loop(0, blocks, mirror, 0, unroll=4)
        parts[1].start(builder(1))
        parts[2].start(builder(2))
        if m:
            totals[1].start(1, totals[1].finish(0))
        else:
            known = gram_of(stack[16:, own_half], stack[16:, own_half])
            totals[3].start(0, fold(known))

        parts[0].receive()
        parts[1].receive()

        def spread(d, carry):
            chunk = received[m, d, pl.ds(0, 32), :].astype(F32)
            for k in range(CAP):
                partners[d * CAP + k] = chunk[8 * k : 8 * k + 8]
            returned[pl.ds(pl.multiple_of(d * 24, 8), 8), :] = chunk[24:32]
            return carry

        lax.fori_loop(0, groups, spread, 0, unroll=4)

        def forward(b, carry):
            low, high = pair_up(partners[where[2 * b]], partners[where[2 * b + 1]])
            left = jnp.concatenate([low, high], axis=0).astype(BF16)
            out = lax.dot_general(left, tiles[b], across, preferred_element_type=F32)
            product[block_rows(b), :] = jnp.concatenate([out[0:8], out[8:16]], axis=1)
            return carry

        lax.fori_loop(0, blocks, forward, 0, unroll=4)
        parts[2].receive()

        def spread_last(d, carry):
            chunk = received[m, d, pl.ds(32, 16), :].astype(F32)
            returned[pl.ds(pl.multiple_of(d * 24 + 8, 8), 16), :] = chunk
            return carry

        lax.fori_loop(0, groups, spread_last, 0, unroll=4)
        for j in range(8):
            added = jnp.zeros((blocks, 128), F32)
            for k in range(CAP):
                rows = returned[pl.ds(8 * k + j, groups, stride=24), :].astype(BF16)
                added = added + jnp.dot(onehot[k], rows, preferred_element_type=F32)
            lines = pl.ds(j, blocks, stride=8)
            product[lines, :] = product[lines, :] + added

        height = blocks * 4
        halves = [pl.ds(pl.multiple_of(s * height, 8), height) for s in (1 - sub, sub)]
        swaps = [pair(2 + 2 * m + i, product.at[h], theirs.at[m, h]) for i, h in enumerate(halves)]
        for one in swaps:
            one.start()
        row = lax.broadcasted_iota(jnp.int32, (16, 16), 0)
        col = lax.broadcasted_iota(jnp.int32, (16, 16), 1)
        eye = jnp.where(row == col, 1.0, 0.0).astype(F32)
        if m:
            qq = unfold(totals[3].finish(1), 16)
            cross = unfold(totals[1].finish(1), 32)
            rr, rq = cross[:, :16], cross[:, 16:]
            first_gram = beside([[rr, rq], [rq.T, qq]])
            alpha = qq - rq.T
            keep = eye - alpha.T
            mix = jnp.concatenate([-eye, keep], axis=1)
            link, inverse = factor(dot_t(dot(mix, first_gram), mix))
            kept = dot(inverse, keep)
            full[...] = dot(jnp.concatenate([-inverse, kept], axis=1), first_stack[...])
            coeffs[0] = alpha
            coeffs[1] = link
            bases[0] = full[own_rows, :] * math.sqrt(nodes)
        else:
            totals[3].start(1, totals[3].finish(0))
        for part in parts:
            part.sent()

        def residual(first):
            def step(t, carry):
                t = first + t
                lanes = pl.ds(pl.multiple_of(t * 128, 128), 128)
                both = []
                for p in range(2):
                    b = 2 * t + p
                    both.append((product[block_rows(b), :] + theirs[m, block_rows(b), :]) * scale_of(b))
                stack[0:8, lanes], stack[8:16, lanes] = pair_up(both[0], both[1])
                return carry

            lax.fori_loop(0, blocks // 4, step, 0, unroll=4)

        swaps[0].wait()
        residual(sub * (blocks // 4))
        totals[m + 1].start(0, fold(gram_of(stack[0:16, own_half], stack[:, own_half])))
        swaps[1].wait()
        residual((1 - sub) * (blocks // 4))
        if not m:
            second_stack[16:48] = first_stack[...]
            continue
        totals[2].start(1, totals[2].finish(0))
        cross = unfold(totals[2].finish(1), 48)
        tt, tr, tq = (cross[:, 16 * k : 16 * k + 16] for k in range(3))
        gram = beside([[tt, tr, tq], [tr.T, rr, rq], [tq.T, rq.T, qq]])
        zero = jnp.zeros((16, 16), F32)
        lift = beside([[-inverse, kept, zero], [zero, -inverse, kept], [zero, zero, eye]])
        gram = dot_t(dot(lift, gram), lift)
        alpha = gram[16:32, 16:32] - gram[16:32, 0:16]
        mix = jnp.concatenate([-eye, eye - alpha.T, -link], axis=1)
        upper, inverse = factor(dot_t(dot(mix, gram), mix))
        coeffs[2] = alpha
        coeffs[3] = upper
        full[...] = dot(dot(dot(inverse, mix), lift), stack[...])
        bases[1] = full[own_rows, :] * math.sqrt(nodes)


def local(sizes, upper_tiles, tile_clusters, cluster_slot, start_block):
    nx, nz, ny = sizes
    blocks, cluster, _ = upper_tiles.shape
    groups = nx * nz * ny
    columns = blocks * cluster
    count = 2 * blocks
    their_start = lax.ppermute(start_block, "sub", [(0, 1), (1, 0)])
    targets = cluster_slot.at[tile_clusters].get(mode="promise_in_bounds").reshape(-1)
    owners = targets // blocks
    order = jnp.arange(count, dtype=jnp.int32)
    before = (owners[:, None] == owners[None, :]) & (order[None, :] < order[:, None])
    where = owners * CAP + jnp.sum(before.astype(jnp.int32), axis=1)
    taken = where[None, :] == jnp.arange(groups * CAP, dtype=jnp.int32)[:, None]
    placed = count - jnp.sum(jnp.where(taken, count - order[None, :], 0), axis=1)
    inside = targets % blocks
    names = jnp.concatenate([inside, jnp.full((1,), blocks, jnp.int32)])
    names = jnp.broadcast_to(names.astype(F32)[:, None], (count + 1, 128))

    dma = pltpu.SemaphoreType.DMA
    block = lambda n: pltpu.VMEM((n, 8, 128), F32)
    wide = lambda *shape: pltpu.VMEM(shape + (128,), F32)
    scratch = [
        pltpu.VMEM((16, columns), F32),
        pltpu.VMEM((32, columns), F32),
        pltpu.VMEM((48, columns), F32),
        block(count + 1),
        wide(groups, CAP),
        wide(groups, CAP),
        wide(blocks),
        wide(blocks),
        wide(blocks),
        wide(blocks),
        pltpu.VMEM((CAP, blocks, groups), BF16),
        pltpu.VMEM((CAP, groups, blocks), BF16),
        wide(blocks * 8 + 8),
        block(count + 1),
        wide(groups * CAP * 8 + CAP * 8),
        pltpu.VMEM((groups, 16 * CAP, 128), BF16),
        pltpu.VMEM((2, groups, 16 * CAP, 128), BF16),
        block(groups * CAP),
        wide(groups * CAP * 8 + CAP * 8),
        wide(blocks * 8 + 8),
        wide(2, blocks * 8),
        wide(4, nx * ny, 8),
        wide(4, nz * 2, 8),
        dma((4, 2)),
        dma((4, 2)),
        dma,
        dma,
        dma,
        dma((6,)),
        dma((6,)),
        dma((2, CAP)),
        dma((2, CAP)),
        dma((2, CAP)),
    ]
    return pl.pallas_call(
        functools.partial(kernel, sizes, blocks, columns * groups),
        out_shape=[
            jax.ShapeDtypeStruct((2, 8, columns), F32),
            jax.ShapeDtypeStruct((4, 16, 16), F32),
        ],
        in_specs=[VMEM, VMEM, VMEM, VMEM, SMEM, SMEM],
        out_specs=[VMEM, VMEM],
        scratch_shapes=scratch,
        compiler_params=pltpu.CompilerParams(collective_id=1, has_side_effects=True, vmem_limit_bytes=LIMIT),
        name="lanczos",
    )(upper_tiles, start_block, their_start, names, placed, where)


def solution(mesh):
    sizes = (4, 8, 4)
    in_specs = (P("rows", None, "sub"), P("rows", "sub"), P(), P("sub", "rows"))
    out_specs = (P(None, "sub", "rows"), P())
    body = functools.partial(local, sizes)
    return jax.shard_map(body, mesh=mesh, in_specs=in_specs, out_specs=out_specs, check_vma=False)
```

```python
import functools
import math

import jax
import jax.numpy as jnp
from jax import lax
from jax.experimental import pallas as pl
from jax.experimental.pallas import tpu as pltpu
from jax.sharding import PartitionSpec as P

CAP = 3
MESH = pl.DeviceIdType.MESH
VMEM = pl.BlockSpec(memory_space=pltpu.VMEM)
SMEM = pl.BlockSpec(memory_space=pltpu.SMEM)
F32 = jnp.float32
BF16 = jnp.bfloat16
LIMIT = 32 << 20
EXACT = lax.Precision.HIGHEST


def dot(left, right):
    return jnp.dot(left, right, precision=EXACT, preferred_element_type=F32)


def dot_t(left, right):
    dims = (((1,), (1,)), ((), ()))
    return lax.dot_general(left, right, dims, precision=EXACT, preferred_element_type=F32)


def swap(x):
    return pltpu.roll(x, 64, 1)


def is_low(shape):
    return lax.broadcasted_iota(jnp.int32, shape, 1) < 64


def pair_up(first, second):
    low = is_low(first.shape)
    return jnp.where(low, first, swap(second)), jnp.where(low, swap(first), second)


class Place:
    def __init__(self, sizes):
        self.nx, self.nz, self.ny = sizes
        self.groups = self.nx * self.nz * self.ny
        self.me, self.sub = lax.axis_index("rows"), lax.axis_index("sub")
        self.x = self.me // (self.nz * self.ny)
        self.z = lax.rem(self.me // self.ny, self.nz)
        self.y = lax.rem(self.me, self.ny)
        self.other = (self.me, 1 - self.sub)
        nx, nz, ny = sizes
        self.plane = [self.at(a, 0, b, 0) for a in range(nx) for b in range(ny)][1:]
        self.line = [self.at(0, a, 0, s) for a in range(nz) for s in range(2)][1:]
        self.slots = (self.x * ny + self.y, self.z * 2 + self.sub)

    def at(self, dx, dz, dy, ds):
        x, z, y = lax.rem(self.x + dx, self.nx), lax.rem(self.z + dz, self.nz), lax.rem(self.y + dy, self.ny)
        return ((x * self.nz + z) * self.ny + y, lax.rem(self.sub + ds, 2))

    def order(self):
        spans = [(0, self.nz // 2)] + [(self.nz // 2 - g, self.nz // 2 + g) for g in range(1, self.nz // 2)]
        wide = 2 * self.nx * self.ny
        for g, (one, two) in enumerate(spans):
            def peer(i, one=one, two=two):
                dz = one + (two - one) * lax.rem(i, 2)
                return self.at(i // (2 * self.ny), dz, lax.rem(i // 2, self.ny), 0)

            yield (1 if g == 0 else 0), wide, peer

    def peer(self, i):
        return (lax.rem(self.me + i, self.groups), self.sub)


def signal(barrier, device):
    pl.semaphore_signal(barrier, inc=1, device_id=device, device_id_type=MESH)


def meet(place, everyone):
    barrier = pltpu.get_barrier_semaphore()
    if everyone:
        def greet(i, carry):
            signal(barrier, place.peer(i))
            return carry

        lax.fori_loop(place.groups // 2, place.groups, greet, 0, unroll=8)
        lax.fori_loop(1, place.groups // 2, greet, 0, unroll=8)
        rest = [d for k, d in enumerate(place.line) if k % 2 == 0]
        count = place.groups - 1 + len(rest)
    else:
        rest = place.plane + place.line
        count = len(rest)
    for device in rest:
        signal(barrier, device)
    return lambda: pl.semaphore_wait(barrier, count)


def remote(src, dst, send_sem, recv_sem, device):
    return pltpu.make_async_remote_copy(
        src_ref=src, dst_ref=dst, send_sem=send_sem, recv_sem=recv_sem, device_id=device, device_id_type=MESH
    )


class Total:
    def __init__(self, place, near, far, send_sem, recv_sem):
        self.hops = ((near, place.slots[0], place.plane), (far, place.slots[1], place.line))
        self.sems = (send_sem, recv_sem)

    def copy(self, k, ref, device):
        return remote(ref, ref, self.sems[0].at[k], self.sems[1].at[k], device)

    def start(self, k, value):
        held, slot, peers = self.hops[k]
        held[pl.ds(slot, 1)] = value[None]
        for device in peers:
            self.copy(k, held.at[slot], device).start()

    def finish(self, k):
        held, _, peers = self.hops[k]
        self.copy(k, held.at[pl.ds(0, len(peers))], peers[0]).wait()
        return jnp.sum(held[...], axis=0)


class Exchange:
    def __init__(self, place, src, dst, send_sem, recv_sem, own_sem, rows=None):
        self.place, self.src, self.dst = place, src, dst
        self.sems, self.own_sem, self.rows = (send_sem, recv_sem), own_sem, rows

    def part(self, ref, i):
        return ref.at[i] if self.rows is None else ref.at[i, self.rows]

    def own(self):
        me = self.place.me
        return pltpu.make_async_copy(self.part(self.src, me), self.part(self.dst, me), self.own_sem)

    def start(self, build, unroll=2):
        place = self.place
        build(place.me)
        self.own().start()
        for begin, end, peer in place.order():
            def send(i, carry):
                device = peer(i)
                build(device[0])
                remote(self.part(self.src, device[0]), self.part(self.dst, place.me), *self.sems, device).start()
                return carry

            lax.fori_loop(begin, end, send, 0, unroll=unroll)

    def rest(self):
        rest = pl.ds(0, self.place.groups - 1)
        return remote(self.part(self.src, rest), self.part(self.dst, rest), *self.sems, self.place.peer(1))

    def receive(self):
        self.own().wait()
        self.rest().wait_recv()

    def sent(self):
        self.rest().wait_send()

def factor(gram):
    n = gram.shape[0]
    row = lax.broadcasted_iota(jnp.int32, (n, n), 0)
    col = lax.broadcasted_iota(jnp.int32, (n, n), 1)
    left = gram
    right = jnp.where(row == col, 1.0, 0.0).astype(F32)
    below = lax.broadcasted_iota(jnp.int32, (n, 1), 0)
    for i in range(n):
        share = jnp.where(below > i, left[:, i : i + 1] / left[i : i + 1, i : i + 1], 0.0)
        right = right - share * right[i : i + 1, :]
        left = left - share * left[i : i + 1, :]
    pivots = jnp.sum(jnp.where(row == col, left, 0.0), axis=1, keepdims=True)
    root = lax.rsqrt(pivots)
    return jnp.where(col >= row, left * root, 0.0), right * root


def fold(x):
    width = x.shape[1]
    return jnp.concatenate([x[0:8], x[8:16], jnp.zeros((8, 128 - 2 * width), F32)], axis=1)


def unfold(x, width):
    return jnp.concatenate([x[:, :width], x[:, width : 2 * width]], axis=0)


def beside(lines):
    return jnp.concatenate([jnp.concatenate(line, axis=1) for line in lines], axis=0)


def pieces(x):
    high = x.astype(BF16)
    rest = x - high.astype(F32)
    middle = rest.astype(BF16)
    return jnp.concatenate([high, middle, (rest - middle.astype(F32)).astype(BF16)], axis=0)


def gram_of(left, right):
    rows, width = left.shape[0], right.shape[0]
    dims = (((1,), (1,)), ((), ()))
    out = lax.dot_general(pieces(left), pieces(right), dims, preferred_element_type=F32)
    out = out[0:rows] + out[rows : 2 * rows] + out[2 * rows :]
    return out[:, :width] + out[:, width : 2 * width] + out[:, 2 * width :]


def kernel(
    sizes, blocks, nodes, tiles, start, their_start, names, placed, where, bases, coeffs,
    full, first_stack, second_stack, named, out_columns, in_columns, own_degree, degree, their_degree, scale,
    onehot, onehot_t, scaled, mirrored, reply, chunks, received, partners, returned, product, theirs,
    near, far, tsend, trecv, csend, crecv, cown, xsend, xrecv, asend, arecv, aown,
):
    place = Place(sizes)
    ready = meet(place, True)
    groups, sub = place.groups, place.sub
    columns = full.shape[1]
    half = columns // 2
    own_half = pl.ds(pl.multiple_of(sub * half, 128), half)
    own_rows = pl.ds(pl.multiple_of(sub * 8, 8), 8)
    totals = [Total(place, near.at[i], far.at[i], tsend.at[i], trecv.at[i]) for i in range(4)]

    def pair(i, src, dst):
        return remote(src, dst, xsend.at[i], xrecv.at[i], place.other)

    full[own_rows, :] = start[...]
    full[pl.ds(pl.multiple_of(8 - sub * 8, 8), 8), :] = their_start[...]
    named[2 * blocks] = jnp.broadcast_to(names[pl.ds(2 * blocks, 1), :], (8, 128))
    mirrored[2 * blocks] = jnp.zeros((8, 128), F32)
    across = (((1,), (1,)), ((), ()))

    def sums(b, carry):
        tile = tiles[b]
        down = jnp.dot(jnp.ones((8, 64), BF16), tile, preferred_element_type=F32)
        low = is_low(down.shape)
        named[2 * b] = jnp.where(low, down, names[pl.ds(2 * b, 1), :])
        named[2 * b + 1] = jnp.where(low, swap(down), names[pl.ds(2 * b + 1, 1), :])
        along = lax.dot_general(jnp.ones((8, 128), BF16), tile, across, preferred_element_type=F32)
        own_degree[pl.ds(b, 1), :] = jnp.concatenate([along, along], axis=1)[0:1]
        return carry

    lax.fori_loop(0, blocks, sums, 0, unroll=4)

    first = fold(gram_of(full[:, own_half], full[:, own_half]))
    ready()
    totals[0].start(0, first)

    def fill(d):
        for k in range(CAP):
            out_columns[d, pl.ds(k, 1), :] = named[placed[CAP * d + k]][0:1]

    sent_columns = Exchange(place, out_columns, in_columns, csend, crecv, cown)
    sent_columns.start(fill, unroll=4)
    totals[0].start(1, totals[0].finish(0))

    sent_columns.receive()
    sums_in = jnp.zeros((blocks, 128), F32)
    for k in range(CAP):
        rows = in_columns[:, k, :]
        index = lax.broadcasted_iota(jnp.int32, (blocks, groups), 0).astype(F32)
        match = jnp.where(index == rows.T[64:65, :], 1.0, 0.0).astype(F32)
        index = lax.broadcasted_iota(jnp.int32, (groups, blocks), 1).astype(F32)
        onehot_t[k] = jnp.where(index == rows[:, 64:65], 1.0, 0.0).astype(BF16)
        onehot[k] = match.astype(BF16)
        sums_in = sums_in + dot(match, rows)
    degree[...] = own_degree[...] + jnp.where(is_low(sums_in.shape), sums_in, swap(sums_in))
    swap_degree = pair(1, degree, their_degree)
    swap_degree.start()
    sent_columns.sent()
    swap_degree.wait()
    scale[...] = lax.rsqrt(degree[...] + their_degree[...])
    _, inverse = factor(unfold(totals[0].finish(1), 16))
    first_stack[16:32] = dot(inverse, full[...])

    def scale_of(b):
        return jnp.broadcast_to(scale[pl.ds(b, 1), :], (8, 128))

    def block_rows(b):
        return pl.ds(pl.multiple_of(b * 8, 8), 8)

    for m, stack in enumerate((first_stack, second_stack)):
        def scale_blocks(t, carry):
            lanes = pl.ds(pl.multiple_of(t * 128, 128), 128)
            pairs = pair_up(stack[16:24, lanes], stack[24:32, lanes])
            for p in range(2):
                scaled[block_rows(2 * t + p), :] = pairs[p] * scale_of(2 * t + p)
            return carry

        if not m:
            lax.fori_loop(0, blocks // 2, scale_blocks, 0, unroll=4)

        def mirror(b, carry):
            block = scaled[block_rows(b), :]
            left = jnp.concatenate([block, swap(block)], axis=0)[:, :64].astype(BF16)
            out = jnp.dot(left, tiles[b], preferred_element_type=F32)
            mirrored[2 * b], mirrored[2 * b + 1] = pair_up(out[0:8], out[8:16])
            return carry

        def answer(slots):
            for j in range(8):
                rows = scaled[pl.ds(j, blocks, stride=8), :].astype(BF16)
                for k in slots:
                    chosen = jnp.dot(onehot_t[k], rows, preferred_element_type=F32)
                    reply[pl.ds(8 * k + j, groups, stride=24), :] = chosen

        def builder(k):
            def build(d):
                if k == 0:
                    value = reply[pl.ds(pl.multiple_of(24 * d, 8), 16), :]
                elif k == 1:
                    last = reply[pl.ds(pl.multiple_of(24 * d + 16, 8), 8), :]
                    value = jnp.concatenate([last, mirrored[placed[CAP * d]]], axis=0)
                else:
                    value = jnp.concatenate([mirrored[placed[CAP * d + s]] for s in (1, 2)], axis=0)
                chunks[d, pl.ds(16 * k, 16), :] = value.astype(BF16)

            return build

        parts = [
            Exchange(
                place, chunks, received.at[m], asend.at[m, k], arecv.at[m, k], aown.at[m, k], pl.ds(16 * k, 16)
            )
            for k in range(CAP)
        ]
        answer((0, 1))
        parts[0].start(builder(0), unroll=4)
        answer((2,))
        lax.fori_loop(0, blocks, mirror, 0, unroll=4)
        parts[1].start(builder(1))
        parts[2].start(builder(2))
        if m:
            totals[1].start(0, fold(gram_of(first_stack[0:16, own_half], first_stack[:, own_half])))
            second_stack[16:48] = first_stack[...]
        else:
            known = gram_of(stack[16:, own_half], stack[16:, own_half])
            totals[3].start(0, fold(known))

        parts[0].receive()
        parts[1].receive()

        def spread(d, carry):
            chunk = received[m, d, pl.ds(0, 32), :].astype(F32)
            for k in range(CAP):
                partners[d * CAP + k] = chunk[8 * k : 8 * k + 8]
            returned[pl.ds(pl.multiple_of(d * 24, 8), 8), :] = chunk[24:32]
            return carry

        lax.fori_loop(0, groups, spread, 0, unroll=4)

        def forward(b, carry):
            low, high = pair_up(partners[where[2 * b]], partners[where[2 * b + 1]])
            left = jnp.concatenate([low, high], axis=0).astype(BF16)
            out = lax.dot_general(left, tiles[b], across, preferred_element_type=F32)
            product[block_rows(b), :] = jnp.concatenate([out[0:8], out[8:16]], axis=1)
            return carry

        lax.fori_loop(0, blocks, forward, 0, unroll=4)
        def scatter(slots):
            for j in range(8):
                added = 0.0
                for k in slots:
                    rows = returned[pl.ds(8 * k + j, groups, stride=24), :].astype(BF16)
                    added = added + jnp.dot(onehot[k], rows, preferred_element_type=F32)
                lines = pl.ds(j, blocks, stride=8)
                product[lines, :] = product[lines, :] + added

        scatter((0,))
        if m:
            totals[1].start(1, totals[1].finish(0))
        parts[2].receive()

        def spread_last(d, carry):
            chunk = received[m, d, pl.ds(32, 16), :].astype(F32)
            returned[pl.ds(pl.multiple_of(d * 24 + 8, 8), 16), :] = chunk
            return carry

        lax.fori_loop(0, groups, spread_last, 0, unroll=4)
        scatter((1, 2))

        height = blocks * 4
        halves = [pl.ds(pl.multiple_of(s * height, 8), height) for s in (1 - sub, sub)]
        swaps = [pair(2 + 2 * m + i, product.at[h], theirs.at[m, h]) for i, h in enumerate(halves)]
        for one in swaps:
            one.start()
        if not m:
            totals[3].start(1, totals[3].finish(0))
        for part in parts:
            part.sent()

        def residual(first):
            def step(t, carry):
                t = first + t
                lanes = pl.ds(pl.multiple_of(t * 128, 128), 128)
                both = []
                for p in range(2):
                    b = 2 * t + p
                    both.append((product[block_rows(b), :] + theirs[m, block_rows(b), :]) * scale_of(b))
                    if not m:
                        scaled[block_rows(b), :] = both[p] * scale_of(b)
                stack[0:8, lanes], stack[8:16, lanes] = pair_up(both[0], both[1])
                return carry

            lax.fori_loop(0, blocks // 4, step, 0, unroll=4)

        swaps[0].wait()
        residual(sub * (blocks // 4))
        if m:
            totals[2].start(0, fold(gram_of(stack[0:16, own_half], stack[:, own_half])))
        swaps[1].wait()
        residual((1 - sub) * (blocks // 4))
        if not m:
            continue
        row = lax.broadcasted_iota(jnp.int32, (16, 16), 0)
        col = lax.broadcasted_iota(jnp.int32, (16, 16), 1)
        eye = jnp.where(row == col, 1.0, 0.0).astype(F32)
        qq = unfold(totals[3].finish(1), 16)
        cross = unfold(totals[1].finish(1), 32)
        rr, rq = cross[:, :16], cross[:, 16:]
        first_gram = beside([[rr, rq], [rq.T, qq]])
        alpha = qq - rq.T
        keep = eye - alpha.T
        mix = jnp.concatenate([-eye, keep], axis=1)
        link, inverse = factor(dot_t(dot(mix, first_gram), mix))
        kept = dot(inverse, keep)
        full[...] = dot(jnp.concatenate([-inverse, kept], axis=1), first_stack[...])
        coeffs[0] = alpha
        coeffs[1] = link
        bases[0] = full[own_rows, :] * math.sqrt(nodes)
        totals[2].start(1, totals[2].finish(0))
        cross = unfold(totals[2].finish(1), 48)
        tt, tr, tq = (cross[:, 16 * k : 16 * k + 16] for k in range(3))
        gram = beside([[tt, tr, tq], [tr.T, rr, rq], [tq.T, rq.T, qq]])
        zero = jnp.zeros((16, 16), F32)
        lift = beside([[-inverse, kept, zero], [zero, -inverse, kept], [zero, zero, eye]])
        gram = dot_t(dot(lift, gram), lift)
        alpha = gram[16:32, 16:32] - gram[16:32, 0:16]
        mix = jnp.concatenate([-eye, eye - alpha.T, -link], axis=1)
        upper, inverse = factor(dot_t(dot(mix, gram), mix))
        coeffs[2] = alpha
        coeffs[3] = upper
        full[...] = dot(dot(dot(inverse, mix), lift), stack[...])
        bases[1] = full[own_rows, :] * math.sqrt(nodes)


def local(sizes, upper_tiles, tile_clusters, cluster_slot, start_block):
    nx, nz, ny = sizes
    blocks, cluster, _ = upper_tiles.shape
    groups = nx * nz * ny
    columns = blocks * cluster
    count = 2 * blocks
    their_start = lax.ppermute(start_block, "sub", [(0, 1), (1, 0)])
    targets = cluster_slot.at[tile_clusters].get(mode="promise_in_bounds").reshape(-1)
    owners = targets // blocks
    order = jnp.arange(count, dtype=jnp.int32)
    before = (owners[:, None] == owners[None, :]) & (order[None, :] < order[:, None])
    where = owners * CAP + jnp.sum(before.astype(jnp.int32), axis=1)
    taken = where[None, :] == jnp.arange(groups * CAP, dtype=jnp.int32)[:, None]
    placed = count - jnp.sum(jnp.where(taken, count - order[None, :], 0), axis=1)
    inside = targets % blocks
    names = jnp.concatenate([inside, jnp.full((1,), blocks, jnp.int32)])
    names = jnp.broadcast_to(names.astype(F32)[:, None], (count + 1, 128))

    dma = pltpu.SemaphoreType.DMA
    block = lambda n: pltpu.VMEM((n, 8, 128), F32)
    wide = lambda *shape: pltpu.VMEM(shape + (128,), F32)
    scratch = [
        pltpu.VMEM((16, columns), F32),
        pltpu.VMEM((32, columns), F32),
        pltpu.VMEM((48, columns), F32),
        block(count + 1),
        wide(groups, CAP),
        wide(groups, CAP),
        wide(blocks),
        wide(blocks),
        wide(blocks),
        wide(blocks),
        pltpu.VMEM((CAP, blocks, groups), BF16),
        pltpu.VMEM((CAP, groups, blocks), BF16),
        wide(blocks * 8 + 8),
        block(count + 1),
        wide(groups * CAP * 8 + CAP * 8),
        pltpu.VMEM((groups, 16 * CAP, 128), BF16),
        pltpu.VMEM((2, groups, 16 * CAP, 128), BF16),
        block(groups * CAP),
        wide(groups * CAP * 8 + CAP * 8),
        wide(blocks * 8 + 8),
        wide(2, blocks * 8),
        wide(4, nx * ny, 8),
        wide(4, nz * 2, 8),
        dma((4, 2)),
        dma((4, 2)),
        dma,
        dma,
        dma,
        dma((6,)),
        dma((6,)),
        dma((2, CAP)),
        dma((2, CAP)),
        dma((2, CAP)),
    ]
    return pl.pallas_call(
        functools.partial(kernel, sizes, blocks, columns * groups),
        out_shape=[
            jax.ShapeDtypeStruct((2, 8, columns), F32),
            jax.ShapeDtypeStruct((4, 16, 16), F32),
        ],
        in_specs=[VMEM, VMEM, VMEM, VMEM, SMEM, SMEM],
        out_specs=[VMEM, VMEM],
        scratch_shapes=scratch,
        compiler_params=pltpu.CompilerParams(collective_id=1, has_side_effects=True, vmem_limit_bytes=LIMIT),
        name="lanczos",
    )(upper_tiles, start_block, their_start, names, placed, where)


def solution(mesh):
    sizes = (4, 8, 4)
    in_specs = (P("rows", None, "sub"), P("rows", "sub"), P(), P("sub", "rows"))
    out_specs = (P(None, "sub", "rows"), P())
    body = functools.partial(local, sizes)
    return jax.shard_map(body, mesh=mesh, in_specs=in_specs, out_specs=out_specs, check_vma=False)
```

```python
import functools
import math

import jax
import jax.numpy as jnp
from jax import lax
from jax.experimental import pallas as pl
from jax.experimental.pallas import tpu as pltpu
from jax.sharding import PartitionSpec as P

CAP = 3
MESH = pl.DeviceIdType.MESH
VMEM = pl.BlockSpec(memory_space=pltpu.VMEM)
SMEM = pl.BlockSpec(memory_space=pltpu.SMEM)
F32 = jnp.float32
BF16 = jnp.bfloat16
LIMIT = 32 << 20
EXACT = lax.Precision.HIGHEST


def dot(left, right):
    return jnp.dot(left, right, precision=EXACT, preferred_element_type=F32)


def dot_t(left, right):
    dims = (((1,), (1,)), ((), ()))
    return lax.dot_general(left, right, dims, precision=EXACT, preferred_element_type=F32)


def swap(x):
    return pltpu.roll(x, 64, 1)


def is_low(shape):
    return lax.broadcasted_iota(jnp.int32, shape, 1) < 64


def pair_up(first, second):
    low = is_low(first.shape)
    return jnp.where(low, first, swap(second)), jnp.where(low, swap(first), second)


class Place:
    def __init__(self, sizes):
        self.nx, self.nz, self.ny = sizes
        self.groups = self.nx * self.nz * self.ny
        self.me, self.sub = lax.axis_index("rows"), lax.axis_index("sub")
        self.x = self.me // (self.nz * self.ny)
        self.z = lax.rem(self.me // self.ny, self.nz)
        self.y = lax.rem(self.me, self.ny)
        self.other = (self.me, 1 - self.sub)
        nx, nz, ny = sizes
        self.plane = [self.at(a, 0, b, 0) for a in range(nx) for b in range(ny)][1:]
        self.line = [self.at(0, a, 0, s) for a in range(nz) for s in range(2)][1:]
        self.slots = (self.x * ny + self.y, self.z * 2 + self.sub)

    def at(self, dx, dz, dy, ds):
        x, z, y = lax.rem(self.x + dx, self.nx), lax.rem(self.z + dz, self.nz), lax.rem(self.y + dy, self.ny)
        return ((x * self.nz + z) * self.ny + y, lax.rem(self.sub + ds, 2))

    def order(self):
        spans = [(0, self.nz // 2)] + [(self.nz // 2 - g, self.nz // 2 + g) for g in range(1, self.nz // 2)]
        wide = 2 * self.nx * self.ny
        for g, (one, two) in enumerate(spans):
            def peer(i, one=one, two=two):
                dz = one + (two - one) * lax.rem(i, 2)
                return self.at(i // (2 * self.ny), dz, lax.rem(i // 2, self.ny), 0)

            yield (1 if g == 0 else 0), wide, peer

    def peer(self, i):
        return (lax.rem(self.me + i, self.groups), self.sub)


def signal(barrier, device):
    pl.semaphore_signal(barrier, inc=1, device_id=device, device_id_type=MESH)


def meet(place, everyone):
    barrier = pltpu.get_barrier_semaphore()
    if everyone:
        def greet(i, carry):
            signal(barrier, place.peer(i))
            return carry

        lax.fori_loop(place.groups // 2, place.groups, greet, 0, unroll=8)
        lax.fori_loop(1, place.groups // 2, greet, 0, unroll=8)
        rest = [d for k, d in enumerate(place.line) if k % 2 == 0]
        count = place.groups - 1 + len(rest)
    else:
        rest = place.plane + place.line
        count = len(rest)
    for device in rest:
        signal(barrier, device)
    return lambda: pl.semaphore_wait(barrier, count)


def remote(src, dst, send_sem, recv_sem, device):
    return pltpu.make_async_remote_copy(
        src_ref=src, dst_ref=dst, send_sem=send_sem, recv_sem=recv_sem, device_id=device, device_id_type=MESH
    )


class Total:
    def __init__(self, place, near, far, send_sem, recv_sem):
        self.hops = ((near, place.slots[0], place.plane), (far, place.slots[1], place.line))
        self.sems = (send_sem, recv_sem)

    def copy(self, k, ref, device):
        return remote(ref, ref, self.sems[0].at[k], self.sems[1].at[k], device)

    def start(self, k, value):
        held, slot, peers = self.hops[k]
        held[pl.ds(slot, 1)] = value[None]
        for device in peers:
            self.copy(k, held.at[slot], device).start()

    def finish(self, k):
        held, _, peers = self.hops[k]
        self.copy(k, held.at[pl.ds(0, len(peers))], peers[0]).wait()
        return jnp.sum(held[...], axis=0)


class Exchange:
    def __init__(self, place, src, dst, send_sem, recv_sem, own_sem, rows=None):
        self.place, self.src, self.dst = place, src, dst
        self.sems, self.own_sem, self.rows = (send_sem, recv_sem), own_sem, rows

    def part(self, ref, i):
        return ref.at[i] if self.rows is None else ref.at[i, self.rows]

    def own(self):
        me = self.place.me
        return pltpu.make_async_copy(self.part(self.src, me), self.part(self.dst, me), self.own_sem)

    def start(self, build, unroll=2):
        place = self.place
        build(place.me)
        self.own().start()
        for begin, end, peer in place.order():
            def send(i, carry):
                device = peer(i)
                build(device[0])
                remote(self.part(self.src, device[0]), self.part(self.dst, place.me), *self.sems, device).start()
                return carry

            lax.fori_loop(begin, end, send, 0, unroll=unroll)

    def rest(self):
        rest = pl.ds(0, self.place.groups - 1)
        return remote(self.part(self.src, rest), self.part(self.dst, rest), *self.sems, self.place.peer(1))

    def receive(self):
        self.own().wait()
        self.rest().wait_recv()

    def sent(self):
        self.rest().wait_send()

def factor(gram):
    n = gram.shape[0]
    row = lax.broadcasted_iota(jnp.int32, (n, n), 0)
    col = lax.broadcasted_iota(jnp.int32, (n, n), 1)
    left = gram
    right = jnp.where(row == col, 1.0, 0.0).astype(F32)
    below = lax.broadcasted_iota(jnp.int32, (n, 1), 0)
    for i in range(n):
        share = jnp.where(below > i, left[:, i : i + 1] / left[i : i + 1, i : i + 1], 0.0)
        right = right - share * right[i : i + 1, :]
        left = left - share * left[i : i + 1, :]
    pivots = jnp.sum(jnp.where(row == col, left, 0.0), axis=1, keepdims=True)
    root = lax.rsqrt(pivots)
    return jnp.where(col >= row, left * root, 0.0), right * root


def fold(x):
    width = x.shape[1]
    return jnp.concatenate([x[0:8], x[8:16], jnp.zeros((8, 128 - 2 * width), F32)], axis=1)


def unfold(x, width):
    return jnp.concatenate([x[:, :width], x[:, width : 2 * width]], axis=0)


def beside(lines):
    return jnp.concatenate([jnp.concatenate(line, axis=1) for line in lines], axis=0)


def pieces(x):
    high = x.astype(BF16)
    rest = x - high.astype(F32)
    middle = rest.astype(BF16)
    return jnp.concatenate([high, middle, (rest - middle.astype(F32)).astype(BF16)], axis=0)


def gram_of(left, right):
    rows, width = left.shape[0], right.shape[0]
    dims = (((1,), (1,)), ((), ()))
    out = lax.dot_general(pieces(left), pieces(right), dims, preferred_element_type=F32)
    out = out[0:rows] + out[rows : 2 * rows] + out[2 * rows :]
    return out[:, :width] + out[:, width : 2 * width] + out[:, 2 * width :]


def kernel(
    sizes, blocks, nodes, tiles, start, their_start, names, placed, where, bases, coeffs,
    full, first_stack, second_stack, named, out_columns, in_columns, own_degree, degree, their_degree, scale,
    onehot, onehot_t, scaled, mirrored, reply, chunks, received, partners, returned, product, theirs,
    near, far, tsend, trecv, csend, crecv, cown, xsend, xrecv, asend, arecv, aown,
):
    place = Place(sizes)
    ready = meet(place, True)
    groups, sub = place.groups, place.sub
    columns = full.shape[1]
    half = columns // 2
    own_half = pl.ds(pl.multiple_of(sub * half, 128), half)
    own_rows = pl.ds(pl.multiple_of(sub * 8, 8), 8)
    totals = [Total(place, near.at[i], far.at[i], tsend.at[i], trecv.at[i]) for i in range(4)]

    def pair(i, src, dst):
        return remote(src, dst, xsend.at[i], xrecv.at[i], place.other)

    full[own_rows, :] = start[...]
    full[pl.ds(pl.multiple_of(8 - sub * 8, 8), 8), :] = their_start[...]
    named[2 * blocks] = jnp.broadcast_to(names[pl.ds(2 * blocks, 1), :], (8, 128))
    mirrored[2 * blocks] = jnp.zeros((8, 128), F32)
    across = (((1,), (1,)), ((), ()))

    def sums(b, carry):
        tile = tiles[b]
        down = jnp.dot(jnp.ones((8, 64), BF16), tile, preferred_element_type=F32)
        low = is_low(down.shape)
        named[2 * b] = jnp.where(low, down, names[pl.ds(2 * b, 1), :])
        named[2 * b + 1] = jnp.where(low, swap(down), names[pl.ds(2 * b + 1, 1), :])
        along = lax.dot_general(jnp.ones((8, 128), BF16), tile, across, preferred_element_type=F32)
        own_degree[pl.ds(b, 1), :] = jnp.concatenate([along, along], axis=1)[0:1]
        return carry

    lax.fori_loop(0, blocks, sums, 0, unroll=4)

    first = fold(gram_of(full[:, own_half], full[:, own_half]))
    ready()
    totals[0].start(0, first)

    def fill(d):
        for k in range(CAP):
            out_columns[d, pl.ds(k, 1), :] = named[placed[CAP * d + k]][0:1]

    sent_columns = Exchange(place, out_columns, in_columns, csend, crecv, cown)
    sent_columns.start(fill, unroll=4)
    totals[0].start(1, totals[0].finish(0))

    sent_columns.receive()
    sums_in = jnp.zeros((blocks, 128), F32)
    for k in range(CAP):
        rows = in_columns[:, k, :]
        index = lax.broadcasted_iota(jnp.int32, (blocks, groups), 0).astype(F32)
        match = jnp.where(index == rows.T[64:65, :], 1.0, 0.0).astype(F32)
        index = lax.broadcasted_iota(jnp.int32, (groups, blocks), 1).astype(F32)
        onehot_t[k] = jnp.where(index == rows[:, 64:65], 1.0, 0.0).astype(BF16)
        onehot[k] = match.astype(BF16)
        sums_in = sums_in + dot(match, rows)
    degree[...] = own_degree[...] + jnp.where(is_low(sums_in.shape), sums_in, swap(sums_in))
    swap_degree = pair(1, degree, their_degree)
    swap_degree.start()
    _, inverse = factor(unfold(totals[0].finish(1), 16))
    first_stack[16:32] = dot(inverse, full[...])
    swap_degree.wait()
    scale[...] = lax.rsqrt(degree[...] + their_degree[...])
    sent_columns.sent()

    def scale_of(b):
        return jnp.broadcast_to(scale[pl.ds(b, 1), :], (8, 128))

    def block_rows(b):
        return pl.ds(pl.multiple_of(b * 8, 8), 8)

    for m, stack in enumerate((first_stack, second_stack)):
        def scale_blocks(t, carry):
            lanes = pl.ds(pl.multiple_of(t * 128, 128), 128)
            pairs = pair_up(stack[16:24, lanes], stack[24:32, lanes])
            for p in range(2):
                scaled[block_rows(2 * t + p), :] = pairs[p] * scale_of(2 * t + p)
            return carry

        if not m:
            lax.fori_loop(0, blocks // 2, scale_blocks, 0, unroll=4)

        def mirror(b, carry):
            block = scaled[block_rows(b), :]
            left = jnp.concatenate([block, swap(block)], axis=0)[:, :64].astype(BF16)
            out = jnp.dot(left, tiles[b], preferred_element_type=F32)
            mirrored[2 * b], mirrored[2 * b + 1] = pair_up(out[0:8], out[8:16])
            return carry

        def answer(slots):
            for j in range(8):
                rows = scaled[pl.ds(j, blocks, stride=8), :].astype(BF16)
                for k in slots:
                    chosen = jnp.dot(onehot_t[k], rows, preferred_element_type=F32)
                    reply[pl.ds(8 * k + j, groups, stride=24), :] = chosen

        def builder(k):
            def build(d):
                if k == 0:
                    value = reply[pl.ds(pl.multiple_of(24 * d, 8), 16), :]
                elif k == 1:
                    last = reply[pl.ds(pl.multiple_of(24 * d + 16, 8), 8), :]
                    value = jnp.concatenate([last, mirrored[placed[CAP * d]]], axis=0)
                else:
                    value = jnp.concatenate([mirrored[placed[CAP * d + s]] for s in (1, 2)], axis=0)
                chunks[d, pl.ds(16 * k, 16), :] = value.astype(BF16)

            return build

        parts = [
            Exchange(
                place, chunks, received.at[m], asend.at[m, k], arecv.at[m, k], aown.at[m, k], pl.ds(16 * k, 16)
            )
            for k in range(CAP)
        ]
        answer((0, 1))
        parts[0].start(builder(0), unroll=4)
        answer((2,))
        lax.fori_loop(0, blocks, mirror, 0, unroll=4)
        parts[1].start(builder(1))
        parts[2].start(builder(2))
        if m:
            totals[1].start(0, fold(gram_of(first_stack[0:16, own_half], first_stack[:, own_half])))
            second_stack[16:48] = first_stack[...]
        else:
            known = gram_of(stack[16:, own_half], stack[16:, own_half])
            totals[3].start(0, fold(known))

        parts[0].receive()
        parts[1].receive()

        def spread(d, carry):
            chunk = received[m, d, pl.ds(0, 32), :].astype(F32)
            for k in range(CAP):
                partners[d * CAP + k] = chunk[8 * k : 8 * k + 8]
            returned[pl.ds(pl.multiple_of(d * 24, 8), 8), :] = chunk[24:32]
            return carry

        lax.fori_loop(0, groups, spread, 0, unroll=4)

        def forward(b, carry):
            low, high = pair_up(partners[where[2 * b]], partners[where[2 * b + 1]])
            left = jnp.concatenate([low, high], axis=0).astype(BF16)
            out = lax.dot_general(left, tiles[b], across, preferred_element_type=F32)
            product[block_rows(b), :] = jnp.concatenate([out[0:8], out[8:16]], axis=1)
            return carry

        lax.fori_loop(0, blocks, forward, 0, unroll=4)
        def scatter(slots):
            for j in range(8):
                added = 0.0
                for k in slots:
                    rows = returned[pl.ds(8 * k + j, groups, stride=24), :].astype(BF16)
                    added = added + jnp.dot(onehot[k], rows, preferred_element_type=F32)
                lines = pl.ds(j, blocks, stride=8)
                product[lines, :] = product[lines, :] + added

        scatter((0,))
        if m:
            totals[1].start(1, totals[1].finish(0))
        parts[2].receive()

        def spread_last(d, carry):
            chunk = received[m, d, pl.ds(32, 16), :].astype(F32)
            returned[pl.ds(pl.multiple_of(d * 24 + 8, 8), 16), :] = chunk
            return carry

        lax.fori_loop(0, groups, spread_last, 0, unroll=4)
        scatter((1, 2))

        height = blocks * 4
        halves = [pl.ds(pl.multiple_of(s * height, 8), height) for s in (1 - sub, sub)]
        swaps = [pair(2 + 2 * m + i, product.at[h], theirs.at[m, h]) for i, h in enumerate(halves)]
        for one in swaps:
            one.start()
        if not m:
            totals[3].start(1, totals[3].finish(0))
        for part in parts:
            part.sent()

        def residual(first):
            def step(t, carry):
                t = first + t
                lanes = pl.ds(pl.multiple_of(t * 128, 128), 128)
                both = []
                for p in range(2):
                    b = 2 * t + p
                    both.append((product[block_rows(b), :] + theirs[m, block_rows(b), :]) * scale_of(b))
                    if not m:
                        scaled[block_rows(b), :] = both[p] * scale_of(b)
                stack[0:8, lanes], stack[8:16, lanes] = pair_up(both[0], both[1])
                return carry

            lax.fori_loop(0, blocks // 4, step, 0, unroll=4)

        swaps[0].wait()
        residual(sub * (blocks // 4))
        if m:
            totals[2].start(0, fold(gram_of(stack[0:16, own_half], stack[:, own_half])))
        swaps[1].wait()
        residual((1 - sub) * (blocks // 4))
        if not m:
            continue
        row = lax.broadcasted_iota(jnp.int32, (16, 16), 0)
        col = lax.broadcasted_iota(jnp.int32, (16, 16), 1)
        eye = jnp.where(row == col, 1.0, 0.0).astype(F32)
        qq = unfold(totals[3].finish(1), 16)
        cross = unfold(totals[1].finish(1), 32)
        rr, rq = cross[:, :16], cross[:, 16:]
        first_gram = beside([[rr, rq], [rq.T, qq]])
        alpha = qq - rq.T
        keep = eye - alpha.T
        mix = jnp.concatenate([-eye, keep], axis=1)
        link, inverse = factor(dot_t(dot(mix, first_gram), mix))
        kept = dot(inverse, keep)
        full[...] = dot(jnp.concatenate([-inverse, kept], axis=1), first_stack[...])
        coeffs[0] = alpha
        coeffs[1] = link
        bases[0] = full[own_rows, :] * math.sqrt(nodes)
        totals[2].start(1, totals[2].finish(0))
        cross = unfold(totals[2].finish(1), 48)
        tt, tr, tq = (cross[:, 16 * k : 16 * k + 16] for k in range(3))
        gram = beside([[tt, tr, tq], [tr.T, rr, rq], [tq.T, rq.T, qq]])
        zero = jnp.zeros((16, 16), F32)
        lift = beside([[-inverse, kept, zero], [zero, -inverse, kept], [zero, zero, eye]])
        gram = dot_t(dot(lift, gram), lift)
        alpha = gram[16:32, 16:32] - gram[16:32, 0:16]
        mix = jnp.concatenate([-eye, eye - alpha.T, -link], axis=1)
        upper, inverse = factor(dot_t(dot(mix, gram), mix))
        coeffs[2] = alpha
        coeffs[3] = upper
        full[...] = dot(dot(dot(inverse, mix), lift), stack[...])
        bases[1] = full[own_rows, :] * math.sqrt(nodes)


def local(sizes, upper_tiles, tile_clusters, cluster_slot, start_block):
    nx, nz, ny = sizes
    blocks, cluster, _ = upper_tiles.shape
    groups = nx * nz * ny
    columns = blocks * cluster
    count = 2 * blocks
    their_start = lax.ppermute(start_block, "sub", [(0, 1), (1, 0)])
    targets = cluster_slot.at[tile_clusters].get(mode="promise_in_bounds").reshape(-1)
    owners = targets // blocks
    order = jnp.arange(count, dtype=jnp.int32)
    before = (owners[:, None] == owners[None, :]) & (order[None, :] < order[:, None])
    where = owners * CAP + jnp.sum(before.astype(jnp.int32), axis=1)
    taken = where[None, :] == jnp.arange(groups * CAP, dtype=jnp.int32)[:, None]
    placed = count - jnp.sum(jnp.where(taken, count - order[None, :], 0), axis=1)
    inside = targets % blocks
    names = jnp.concatenate([inside, jnp.full((1,), blocks, jnp.int32)])
    names = jnp.broadcast_to(names.astype(F32)[:, None], (count + 1, 128))

    dma = pltpu.SemaphoreType.DMA
    block = lambda n: pltpu.VMEM((n, 8, 128), F32)
    wide = lambda *shape: pltpu.VMEM(shape + (128,), F32)
    scratch = [
        pltpu.VMEM((16, columns), F32),
        pltpu.VMEM((32, columns), F32),
        pltpu.VMEM((48, columns), F32),
        block(count + 1),
        wide(groups, CAP),
        wide(groups, CAP),
        wide(blocks),
        wide(blocks),
        wide(blocks),
        wide(blocks),
        pltpu.VMEM((CAP, blocks, groups), BF16),
        pltpu.VMEM((CAP, groups, blocks), BF16),
        wide(blocks * 8 + 8),
        block(count + 1),
        wide(groups * CAP * 8 + CAP * 8),
        pltpu.VMEM((groups, 16 * CAP, 128), BF16),
        pltpu.VMEM((2, groups, 16 * CAP, 128), BF16),
        block(groups * CAP),
        wide(groups * CAP * 8 + CAP * 8),
        wide(blocks * 8 + 8),
        wide(2, blocks * 8),
        wide(4, nx * ny, 8),
        wide(4, nz * 2, 8),
        dma((4, 2)),
        dma((4, 2)),
        dma,
        dma,
        dma,
        dma((6,)),
        dma((6,)),
        dma((2, CAP)),
        dma((2, CAP)),
        dma((2, CAP)),
    ]
    return pl.pallas_call(
        functools.partial(kernel, sizes, blocks, columns * groups),
        out_shape=[
            jax.ShapeDtypeStruct((2, 8, columns), F32),
            jax.ShapeDtypeStruct((4, 16, 16), F32),
        ],
        in_specs=[VMEM, VMEM, VMEM, VMEM, SMEM, SMEM],
        out_specs=[VMEM, VMEM],
        scratch_shapes=scratch,
        compiler_params=pltpu.CompilerParams(collective_id=1, has_side_effects=True, vmem_limit_bytes=LIMIT),
        name="lanczos",
    )(upper_tiles, start_block, their_start, names, placed, where)


def solution(mesh):
    sizes = (4, 8, 4)
    in_specs = (P("rows", None, "sub"), P("rows", "sub"), P(), P("sub", "rows"))
    out_specs = (P(None, "sub", "rows"), P())
    body = functools.partial(local, sizes)
    return jax.shard_map(body, mesh=mesh, in_specs=in_specs, out_specs=out_specs, check_vma=False)
```
